256 devices in a mesh: pts: 32 (over x, z), dp: 8 (over y, core).
Axes of the slice: x: 4, y: 4, z: 8, core: 2. Of those that a mesh axis runs over, the one named last changes fastest.
Arguments:
- features: bfloat16 [131072, 256], P(('dp', 'pts')), parts along dimension 0, may hold values from -640 to 640
- morton_order: int32 [131072], P(('dp', 'pts')), parts along dimension 0, may hold values from 0 to 16383, as said below
- hilbert_order: int32 [131072], P(('dp', 'pts')), parts along dimension 0, may hold values from 0 to 16383, as said below
- cotangent: bfloat16 [131072, 256], P(('dp', 'pts')), parts along dimension 0, may hold values from -6 to 6
- norm_gains: bfloat16 [2, 2, 256], replicated, may hold values from 0.099609375 to 1.8984375
- qkv_weight: bfloat16 [2, 256, 768], replicated, may hold values from -0.375 to 0.375
- proj_weight: bfloat16 [2, 256, 256], replicated, may hold values from -0.375 to 0.375
- expand_weight: bfloat16 [2, 256, 1024], replicated, may hold values from -0.375 to 0.375
- contract_weight: bfloat16 [2, 1024, 256], replicated, may hold values from -0.1875 to 0.1875
Outputs:
- block_output: bfloat16 [131072, 256], P(('dp', 'pts')), parts along dimension 0
- feature_grad: bfloat16 [131072, 256], P(('dp', 'pts')), parts along dimension 0
- gain_grad: float32 [16, 256], P('dp', 'pts'), parts along dimension 0
- qkv_grad: float32 [2048, 768], P(('dp', 'pts')), parts along dimension 0
- proj_grad: float32 [2048, 256], P(('dp', 'pts')), parts along dimension 0
- expand_grad: float32 [2048, 1024], P(('dp', 'pts')), parts along dimension 0
- contract_grad: float32 [8192, 256], P(('dp', 'pts')), parts along dimension 0
The draws below stay inside these ranges and needn't reach their ends.
There are 8 independent parts, one for each index of `dp`. The reference program is written for one: setup_inputs(seed, part) draws one part's arguments, and reference() takes and returns one part's arrays. A program takes and returns all parts, laid end to end along the dimension named above; an argument that names none is the same for every part. Nothing has to cross between parts.
Inputs may be any that keep to these rules, and one draw needn't show every extreme that they name: A permutation of the stored rows: Z-order position j holds stored row morton_order[j]. With positions and stored rows taken in aligned blocks of 512, each block of positions takes 1 to 31 rows from each block of stored rows, exactly 31 for some pairs in every draw, and the counts from each block of stored rows to the blocks of positions are a rearrangement of one list. A permutation of the Z-order positions: Hilbert position j holds Z-order position hilbert_order[j]. The same bounds hold between aligned blocks of 512 Hilbert positions and of 512 Z-order positions.
All inputs are finite; a program needn't handle non-finite values.
Results may differ from the reference program's by a relative error of at most 0.034.
Values may be sent and summed in bfloat16 or wider, within the bound.
A program may use at most 128 MiB of HBM per device.

```python
import math
import jax
import jax.numpy as jnp
from jax import lax

D = 256
HEADS = 8
FF = 1024
PATCH = 512
ROWS = 512
HD = 32
POINTS = 16384


def arrangement(key):
    peer_total = POINTS // ROWS
    mean_count = ROWS // peer_total
    slot_cap = 2 * mean_count - 1
    subkeys = jax.random.split(key, 5)
    rank_of = jax.random.permutation(subkeys[0], peer_total).astype(jnp.int32)
    offsets = jax.random.permutation(subkeys[1], peer_total).astype(jnp.int32)
    shifts = jax.random.randint(subkeys[2], (peer_total // 2,), mean_count - slot_cap, slot_cap - mean_count + 1, dtype=jnp.int32)
    shifts = shifts.at[0].set(slot_cap - mean_count)
    weights = jnp.full((peer_total,), mean_count, jnp.int32)
    weights = weights.at[offsets[0::2]].add(shifts).at[offsets[1::2]].add(-shifts)
    counts = weights[(rank_of[None, :] - rank_of[:, None]) % peer_total]
    row_start = jnp.cumsum(counts, axis=1) - counts
    col_end = jnp.cumsum(counts, axis=0)
    col_start = col_end - counts
    targets = jnp.arange(ROWS, dtype=jnp.int32)
    dest_ids = jnp.arange(peer_total, dtype=jnp.int32)[:, None]
    source = jnp.sum((col_end.T[:, None, :] <= targets[None, :, None]).astype(jnp.int32), axis=2)
    offset_in = targets[None, :] - col_start[source, dest_ids]
    source_slot = row_start[source, dest_ids] + offset_in

    def shuffle(one_key):
        return jax.random.permutation(one_key, ROWS).astype(jnp.int32)
    source_perm = jax.vmap(shuffle)(jax.random.split(subkeys[3], peer_total))
    dest_perm = jax.vmap(shuffle)(jax.random.split(subkeys[4], peer_total))
    values = source * ROWS + source_perm[source, source_slot]
    positions = dest_ids * ROWS + dest_perm[dest_ids, targets[None, :]]
    ordering = jnp.zeros((POINTS,), jnp.int32).at[positions.reshape(-1)].set(values.reshape(-1))
    return ordering


def draw_morton_order(key, part):
    key = jax.random.fold_in(key, 3)
    return arrangement(key)


def draw_hilbert_order(key, part):
    key = jax.random.fold_in(key, 5)
    return arrangement(key)


def draw_features(key, part):
    key = jax.random.fold_in(key, 7)
    subkeys = jax.random.split(key, 4)
    col_scale = jnp.exp(jax.random.uniform(subkeys[1], (1, D), jnp.float32, 0.0, math.log(10.0)))
    row_scale = jnp.exp(jax.random.uniform(subkeys[0], (POINTS, 1), jnp.float32, 0.0, math.log(10.0)))
    base = jnp.clip(jax.random.normal(subkeys[3], (POINTS, D), jnp.float32), -4.0, 4.0)
    return (base * row_scale * col_scale).astype(jnp.bfloat16)


def shard_levels(stream_key, extent, pieces, smallest, high):
    def one(position, blocks):
        heights = jax.random.uniform(jax.random.fold_in(jax.random.fold_in(stream_key, 6), position), (blocks,), jnp.float32, smallest / len(pieces), high / len(pieces))
        return jnp.repeat(jnp.exp(heights), extent[position] // blocks).reshape((-1,) + (1,) * (len(extent) - position - 1))

    factor_of = one(*pieces[0])
    for cut in pieces[1:]:
        factor_of = factor_of * one(*cut)
    return factor_of


def gaussian(stream_key, shape, deviation, most, pieces=(), kind=jnp.bfloat16):
    level = shard_levels(stream_key, shape, pieces, -0.22, 0.18) if pieces else 1.0
    entries = jax.random.normal(stream_key, shape, jnp.float32) * deviation * level
    return jnp.minimum(jnp.maximum(entries, -most), most).astype(kind)


def setup_inputs(seed: int = 0, part: int = 0) -> dict:
    streams_of = jax.random.split(jax.random.key(seed), 10)
    part_splits = jax.random.split(jax.random.fold_in(streams_of[9], part), 10)
    return {
        "features": draw_features(jax.random.fold_in(jax.random.fold_in(streams_of[9], part), 71), part),
        "morton_order": draw_morton_order(jax.random.fold_in(jax.random.fold_in(streams_of[9], part), 71), part),
        "hilbert_order": draw_hilbert_order(jax.random.fold_in(jax.random.fold_in(streams_of[9], part), 71), part),
        "cotangent": gaussian(part_splits[3], (POINTS, D), 1.0, 6.0, ((0, 32),)),
        "norm_gains": jnp.clip(1.0 + 0.18 * jax.random.normal(streams_of[4], (2, 2, D), jnp.float32), 0.099609375, 1.8984375).astype(jnp.bfloat16),
        "qkv_weight": gaussian(streams_of[5], (2, D, 3 * D), D ** -0.5, 0.375),
        "proj_weight": gaussian(streams_of[6], (2, D, D), D ** -0.5, 0.375),
        "expand_weight": gaussian(streams_of[7], (2, D, FF), D ** -0.5, 0.375),
        "contract_weight": gaussian(streams_of[8], (2, FF, D), FF ** -0.5, 0.1875),
    }


def layer_norm(values, gain):
    center = values - lax.optimization_barrier(jnp.mean(values, axis=-1, keepdims=True))
    spread = lax.optimization_barrier(jnp.mean(center * center, axis=-1, keepdims=True))
    return center * lax.rsqrt(spread + 1e-05) * gain.astype(jnp.float32)

def patch_attention(packed):
    query = packed[:, 0].astype(jnp.float32)
    key_rows = packed[:, 1].astype(jnp.float32)
    value_rows = packed[:, 2].astype(jnp.float32)
    scores = jnp.einsum('qhd,khd->hqk', query, key_rows) * HD ** (-0.5)
    expon = jnp.exp(scores)
    attn = (expon / lax.optimization_barrier(jnp.sum(expon, axis=-1, keepdims=True))).astype(jnp.bfloat16)
    mixed = jnp.einsum('hqk,khd->qhd', attn.astype(jnp.float32), value_rows)
    return mixed.astype(jnp.bfloat16).reshape(PATCH, D)

def block_apply(point_rows, params):
    gains, qkv_w, proj_w, expand_w, contract_w = params
    resid = point_rows.astype(jnp.float32)
    normed = layer_norm(resid, gains[0]).astype(jnp.bfloat16)
    packed = jnp.dot(normed, qkv_w, preferred_element_type=jnp.float32).astype(jnp.bfloat16)
    packed = packed.reshape(-1, PATCH, 3, HEADS, HD)
    mixed = lax.map(patch_attention, packed).reshape(-1, D)
    after_attn = resid + jnp.dot(mixed, proj_w, preferred_element_type=jnp.float32)
    normed_two = layer_norm(after_attn, gains[1]).astype(jnp.bfloat16)
    hidden = jax.nn.gelu(jnp.dot(normed_two, expand_w, preferred_element_type=jnp.float32), approximate=False).astype(jnp.bfloat16)
    return (after_attn + jnp.dot(hidden, contract_w, preferred_element_type=jnp.float32)).astype(jnp.bfloat16)

def forward_groups(point_rows, params):
    groups = point_rows.reshape(POINTS // ROWS, ROWS, D)

    def one_group(group_rows):
        return block_apply(group_rows, params)
    return lax.map(one_group, groups).reshape(POINTS, D)

def backward_groups(point_rows, params, upstream):
    groups = point_rows.reshape(POINTS // ROWS, ROWS, D)
    cot_groups = upstream.reshape(POINTS // ROWS, ROWS, D)

    def accumulate(totals, pair_item):
        group_rows, cot_rows = pair_item
        result, pullback = jax.vjp(block_apply, group_rows, params)
        row_grad, param_grads = pullback(cot_rows)
        totals = tuple((total + partial_grad.astype(jnp.float32) for total, partial_grad in zip(totals, param_grads)))
        return (totals, row_grad)
    initial = tuple((jnp.zeros(param.shape, jnp.float32) for param in params))
    totals, row_grads = lax.scan(accumulate, initial, (groups, cot_groups))
    return (row_grads.reshape(POINTS, D), totals)

def backward_rows_only(point_rows, params, upstream):
    groups = point_rows.reshape(POINTS // ROWS, ROWS, D)
    cot_groups = upstream.reshape(POINTS // ROWS, ROWS, D)

    def one_group(pair_item):
        group_rows, cot_rows = pair_item

        def apply_rows(rows_in):
            return block_apply(rows_in, params)
        result, pullback = jax.vjp(apply_rows, group_rows)
        return pullback(cot_rows)[0]
    return lax.map(one_group, (groups, cot_groups)).reshape(POINTS, D)

def reference(features, morton_order, hilbert_order, cotangent, norm_gains, qkv_weight, proj_weight, expand_weight, contract_weight):
    stacked = (norm_gains, qkv_weight, proj_weight, expand_weight, contract_weight)
    first_params = tuple((weight_set[0] for weight_set in stacked))
    second_params = tuple((weight_set[1] for weight_set in stacked))
    morton_rows = jnp.take(features, morton_order, axis=0)
    morton_out = forward_groups(morton_rows, first_params)
    hilbert_rows = jnp.take(morton_out, hilbert_order, axis=0)
    block_output = forward_groups(hilbert_rows, second_params)
    hilbert_grad, second_grads = backward_groups(hilbert_rows, second_params, cotangent)
    morton_grad = jnp.zeros_like(morton_out).at[hilbert_order].set(hilbert_grad)
    morton_row_grad = backward_rows_only(morton_rows, first_params, morton_grad)
    feature_grad = jnp.zeros_like(features).at[morton_order].set(morton_row_grad)
    return (block_output, feature_grad, second_grads[0], second_grads[1], second_grads[2], second_grads[3], second_grads[4])
```

```python
import functools
import math

import jax
import jax.numpy as jnp
from jax import lax
from jax.experimental import pallas as pl
from jax.experimental.pallas import tpu as pltpu
from jax.sharding import PartitionSpec as P

f32, bf16 = jnp.float32, jnp.bfloat16
MESH = pl.DeviceIdType.MESH
D, HEADS, FF, HD = 256, 8, 1024, 32
N = 512
NX, NZ = 4, 8
PEERS = NX * NZ
SLOT = 32
SLOTS = PEERS * SLOT
WIDE = 1664
SCALE = HD**-0.5
LOG2E = math.log2(math.e)


def nn(a, b):
    return jnp.dot(a, b, preferred_element_type=f32)


def nt(a, b):
    return lax.dot_general(a, b, (((1,), (1,)), ((), ())), preferred_element_type=f32)


def iota(shape, axis):
    return lax.broadcasted_iota(jnp.int32, shape, axis)


def one_hot(condition):
    return jnp.where(condition, 1.0, 0.0).astype(bf16)


def norm_stats(x):
    center = x - jnp.mean(x, axis=0, keepdims=True)
    r = lax.rsqrt(jnp.mean(center * center, axis=0, keepdims=True) + 1e-5)
    return center * r, r


def norm_back(dn, xh, r, gain):
    dxh = dn * gain
    m1 = jnp.mean(dxh, axis=0, keepdims=True)
    m2 = jnp.mean(dxh * xh, axis=0, keepdims=True)
    return r * (dxh - m1 - xh * m2)


def heads_loop(head, per=2):
    def body(i, c):
        for k in range(per):
            head(i * per + k)
        return c

    lax.fori_loop(0, HEADS // per, body, 0)


def forward(x, s, b):
    xh, r = norm_stats(x)
    s.xh1[b] = xh
    s.r1[b] = r
    n1 = (xh * s.gain[2 * b][:, 0:1]).astype(bf16)
    s.n1[b] = n1
    s.qkv[b] = nn(s.qkv_t[b], n1).astype(bf16)
    s.kv[b] = nn(n1.T, s.qkv_w[b][:, D:]).astype(bf16)

    def head(h):
        rows = pl.multiple_of(h * HD, HD)
        keys = s.kv[b, :, :D] * s.mask[pl.ds(h, 1), :].astype(bf16)
        scores = nn(keys, s.qkv[b, :D, :])
        e = jnp.exp2(scores * (SCALE * LOG2E))
        p = (e * (1.0 / jnp.sum(e, axis=0, keepdims=True))).astype(bf16)
        s.attn[b, h] = p
        s.mix[b, pl.ds(rows, HD), :] = nn(s.qkv[b, pl.ds(rows + 2 * D, HD), :], p).astype(bf16)

    heads_loop(head)
    a = x + nn(s.proj_t[b], s.mix[b])
    xh2, r2 = norm_stats(a)
    s.xh2[b] = xh2
    s.r2[b] = r2
    n2 = (xh2 * s.gain[2 * b + 1][:, 0:1]).astype(bf16)
    s.n2[b] = n2
    u = nn(s.exp_t[b], n2)
    cdf = 0.5 + 0.5 * lax.erf(u * (0.5**0.5))
    hid = (u * cdf).astype(bf16)
    s.u[b] = u
    s.cdf[b] = cdf
    s.hid[b] = hid
    return (a + nn(s.con_t[b], hid)).astype(bf16)


def gelu_slope(s, b):
    u = s.u[b]
    s.u[b] = s.cdf[b] + u * (jnp.exp2(u * u * (-0.5 * LOG2E)) * (1 / math.sqrt(2 * math.pi)))


def backward(dy, s, b):
    du = (nn(s.con_w[b], dy).astype(bf16).astype(f32) * s.u[b]).astype(bf16)
    s.du[...] = du
    dn2 = nn(s.exp_w[b], du).astype(bf16).astype(f32)
    s.dn2[...] = dn2
    da = dy.astype(f32) + norm_back(dn2, s.xh2[b], s.r2[b], s.gain[2 * b + 1][:, 0:1])
    dab = da.astype(bf16)
    s.dab[...] = dab
    s.dmix[...] = nn(s.proj_w[b], dab).astype(bf16)

    def head(h):
        rows = pl.multiple_of(h * HD, HD)
        do = s.dmix[pl.ds(rows, HD), :]
        mixed = s.mix[b, pl.ds(rows, HD), :].astype(f32)
        delta = jnp.sum(do.astype(f32) * mixed, axis=0, keepdims=True)
        p = s.attn[b, h]
        values = s.kv[b, :, D:] * s.mask[pl.ds(h, 1), :].astype(bf16)
        ds = (p.astype(f32) * (nn(values, s.dmix[...]) - delta)).astype(bf16)
        query, key = s.qkv[b, pl.ds(rows, HD), :], s.qkv[b, pl.ds(rows + D, HD), :]
        s.dqkv[pl.ds(rows + 2 * D, HD), :] = nt(do, p).astype(bf16)
        s.dqkv[pl.ds(rows + D, HD), :] = (nt(query, ds) * SCALE).astype(bf16)
        s.dqkv[pl.ds(rows, HD), :] = (nn(key, ds) * SCALE).astype(bf16)

    heads_loop(head)
    dn1 = nn(s.qkv_w[b], s.dqkv[...]).astype(bf16).astype(f32)
    s.dn1[...] = dn1
    return (da + norm_back(dn1, s.xh1[b], s.r1[b], s.gain[2 * b][:, 0:1])).astype(bf16)


def weight_grads(dy, s):
    qkv = nt(s.n1[1], s.dqkv[...])
    proj = nt(s.mix[1], s.dab[...])
    first = jnp.concatenate([qkv, proj], axis=1).reshape(PEERS, 8, FF)
    second = nt(s.n2[1], s.du[...]).reshape(PEERS, 8, FF)
    s.grads[:, :, :FF] = jnp.concatenate([first, second], axis=1).astype(bf16)
    contract = nt(s.hid[1], dy).astype(bf16).reshape(PEERS, 32, D)
    s.grads[:, :, FF : FF + D] = contract[:, :16]
    s.grads[:, :, FF + D : FF + 2 * D] = contract[:, 16:]
    g1 = jnp.sum(s.dn1[...] * s.xh1[1], axis=1, keepdims=True)
    g2 = jnp.sum(s.dn2[...] * s.xh2[1], axis=1, keepdims=True)
    lane = iota((D, 128), 1)
    gains = jnp.where(lane == 0, g1, jnp.where(lane == 1, g2, 0.0)).reshape(PEERS, 8, 128)
    s.grads[:, :, FF + 2 * D :] = jnp.concatenate([gains, jnp.zeros_like(gains)], axis=1).astype(bf16)


def plan(order, shift):
    source, local = order // N, order % N
    member = one_hot(source == iota((PEERS, N), 0))
    before = one_hot(iota((N, N), 0) < iota((N, N), 1))
    rank = jnp.sum(member.astype(f32) * nn(member, before), axis=0, keepdims=True).astype(jnp.int32)
    at_slot = one_hot(rank + shift == iota((128, N), 0))
    wanted = local + 1
    high, low = (wanted // 256).astype(f32).astype(bf16), (wanted % 256).astype(f32).astype(bf16)
    asked = nt(member * high, at_slot) * 256.0 + nt(member * low, at_slot)
    return source * SLOT + rank, asked


def pack_matrix(asked, shift):
    at = iota((PEERS, SLOT, 128), 2) == iota((PEERS, SLOT, 128), 1) + shift
    column = jnp.sum(jnp.where(at, asked, 0.0), axis=2, keepdims=True).astype(jnp.int32)
    return one_hot(column == iota((PEERS, SLOT, N), 2) + 1).reshape(SLOTS, N)


class State:
    pass


SCRATCH = dict(
    mask=pltpu.VMEM((HEADS, D), f32),
    gain=pltpu.VMEM((4, D, 128), f32),
    xh1=pltpu.VMEM((2, D, N), f32),
    r1=pltpu.VMEM((2, 1, N), f32),
    xh2=pltpu.VMEM((2, D, N), f32),
    r2=pltpu.VMEM((2, 1, N), f32),
    n1=pltpu.VMEM((2, D, N), bf16),
    n2=pltpu.VMEM((2, D, N), bf16),
    qkv=pltpu.VMEM((2, 3 * D, N), bf16),
    kv=pltpu.VMEM((2, N, 2 * D), bf16),
    attn=pltpu.VMEM((2, HEADS, N, N), bf16),
    mix=pltpu.VMEM((2, D, N), bf16),
    u=pltpu.VMEM((2, FF, N), f32),
    cdf=pltpu.VMEM((2, FF, N), f32),
    hid=pltpu.VMEM((2, FF, N), bf16),
    du=pltpu.VMEM((FF, N), bf16),
    dab=pltpu.VMEM((D, N), bf16),
    dn1=pltpu.VMEM((D, N), f32),
    dn2=pltpu.VMEM((D, N), f32),
    dmix=pltpu.VMEM((D, N), bf16),
    dqkv=pltpu.VMEM((3 * D, N), bf16),
    qkv_t=pltpu.VMEM((2, 3 * D, D), bf16),
    proj_t=pltpu.VMEM((2, D, D), bf16),
    exp_t=pltpu.VMEM((2, FF, D), bf16),
    con_t=pltpu.VMEM((2, D, FF), bf16),
    cot_t=pltpu.VMEM((D, N), bf16),
    pack=pltpu.VMEM((2, SLOTS, N), bf16),
    place=pltpu.VMEM((2, SLOTS, N), bf16),
    ask_out=pltpu.VMEM((PEERS, 1, 128), f32),
    ask_in=pltpu.VMEM((PEERS, 1, 128), f32),
    out=pltpu.VMEM((4, PEERS, SLOT, D), bf16),
    inc=pltpu.VMEM((4, PEERS, SLOT, D), bf16),
    grads=pltpu.VMEM((PEERS, 16, WIDE), bf16),
    grads_x=pltpu.VMEM((NX, NZ, 16, WIDE), bf16),
    part=pltpu.VMEM((NZ, 16, WIDE), bf16),
    grads_z=pltpu.VMEM((NZ, 16, WIDE), bf16),
    ask_send=pltpu.SemaphoreType.DMA((PEERS,)),
    ask_recv=pltpu.SemaphoreType.DMA((PEERS,)),
    row_send=pltpu.SemaphoreType.DMA((4, PEERS)),
    row_recv=pltpu.SemaphoreType.DMA((4, PEERS)),
    x_send=pltpu.SemaphoreType.DMA((NX,)),
    x_recv=pltpu.SemaphoreType.DMA((NX,)),
    z_send=pltpu.SemaphoreType.DMA((NZ,)),
    z_recv=pltpu.SemaphoreType.DMA((NZ,)),
)


def kernel(
    morton_ref,
    hilbert_ref,
    features_ref,
    cotangent_ref,
    gains_ref,
    qkv_ref,
    proj_ref,
    expand_ref,
    contract_ref,
    block_ref,
    feature_ref,
    gain_ref,
    dqkv_ref,
    dproj_ref,
    dexpand_ref,
    dcontract_ref,
    *scratch,
):
    s = State()
    for name, ref in zip(SCRATCH, scratch):
        setattr(s, name, ref)
    s.qkv_w, s.proj_w, s.exp_w, s.con_w = qkv_ref, proj_ref, expand_ref, contract_ref
    me = lax.axis_index("pts")
    my_x, my_z = me // NZ, me % NZ

    def toward(k):
        return (my_x + k // NZ) % NX * NZ + (my_z + k % NZ) % NZ

    def origin(k):
        return (my_x + NX - k // NZ) % NX * NZ + (my_z + NZ - k % NZ) % NZ

    def loop(body):
        def one(k, c):
            body(k)
            return c

        lax.fori_loop(1, PEERS, one, 0)

    def copy(src, dst, send_sem, recv_sem, to):
        return pltpu.make_async_remote_copy(
            src_ref=src,
            dst_ref=dst,
            send_sem=send_sem,
            recv_sem=recv_sem,
            device_id={"pts": to},
            device_id_type=MESH,
        )

    def ask_copy(k, slot):
        to = toward(k)
        return copy(s.ask_out.at[to], s.ask_in.at[slot], s.ask_send.at[k], s.ask_recv.at[k], to)

    def row_copy(e, k, slot):
        to = toward(k)
        return copy(s.out.at[e, to], s.inc.at[e, slot], s.row_send.at[e, k], s.row_recv.at[e, k], to)

    def send_rows(e, rows):
        s.out[e] = rows.astype(bf16).reshape(PEERS, SLOT, D)
        loop(lambda k: row_copy(e, k, me).start())
        s.inc[e, me] = s.out[e, me]

    def received(e):
        loop(lambda k: row_copy(e, k, origin(k)).wait_recv())
        return s.inc[e].reshape(SLOTS, D).T

    barrier = pltpu.get_barrier_semaphore()
    loop(lambda k: pl.semaphore_signal(barrier, inc=1, device_id={"pts": toward(k)}, device_id_type=MESH))

    places = []
    asked = jnp.zeros((PEERS, 128), f32)
    for i, order_ref in enumerate((morton_ref, hilbert_ref)):
        place, wanted = plan(order_ref[...], i * SLOT)
        places.append(place)
        asked = asked + wanted
    for p in range(PEERS):
        s.ask_out[p] = asked[p : p + 1, :]
    pl.semaphore_wait(barrier, PEERS - 1)
    loop(lambda k: ask_copy(k, me).start())
    s.ask_in[me] = s.ask_out[me]

    for i in range(2):
        s.place[i] = one_hot(places[i] == iota((SLOTS, N), 0))
    s.mask[...] = jnp.where(iota((HEADS, D), 1) // HD == iota((HEADS, D), 0), 1.0, 0.0)
    for i in range(4):
        row = gains_ref[i // 2, i % 2 : i % 2 + 1, :].astype(f32)
        s.gain[i] = jnp.broadcast_to(row, (128, D)).T

    def transpose_weights(b):
        s.qkv_t[b] = qkv_ref[b].T
        s.proj_t[b] = proj_ref[b].T
        s.exp_t[b] = expand_ref[b].T
        s.con_t[b] = contract_ref[b].T

    loop(lambda k: ask_copy(k, origin(k)).wait_recv())
    s.pack[0] = pack_matrix(s.ask_in[...], 0)
    send_rows(0, nn(s.pack[0], features_ref[...]))
    transpose_weights(0)
    transpose_weights(1)
    s.pack[1] = pack_matrix(s.ask_in[...], SLOT)
    s.cot_t[...] = cotangent_ref[...].T

    morton_rows = nn(received(0), s.place[0])
    morton_out = forward(morton_rows, s, 0)
    send_rows(1, nt(s.pack[1], morton_out))
    gelu_slope(s, 0)

    hilbert_rows = nn(received(1), s.place[1])
    out = forward(hilbert_rows, s, 1)
    block_ref[...] = out.T
    gelu_slope(s, 1)
    hilbert_grad = backward(s.cot_t[...], s, 1)
    send_rows(2, nt(s.place[1], hilbert_grad))

    weight_grads(s.cot_t[...], s)

    def x_copy(k):
        x = (my_x + k) % NX
        slab = s.grads.at[pl.ds(pl.multiple_of(x * NZ, NZ), NZ)]
        return copy(slab, s.grads_x.at[k], s.x_send.at[k], s.x_recv.at[k], x * NZ + my_z)

    def z_copy(k):
        z = (my_z + k) % NZ
        return copy(s.part.at[z], s.grads_z.at[k], s.z_send.at[k], s.z_recv.at[k], my_x * NZ + z)

    for k in range(1, NX):
        x_copy(k).start()

    morton_grad = nn(received(2), s.pack[1]).astype(bf16)
    morton_row_grad = backward(morton_grad, s, 0)
    send_rows(3, nt(s.place[0], morton_row_grad))

    for k in range(1, NX):
        x_copy(k).wait_recv()
    total = s.grads[pl.ds(pl.multiple_of(my_x * NZ, NZ), NZ)].astype(f32)
    for k in range(1, NX):
        total = total + s.grads_x[k].astype(f32)
    s.part[...] = total.astype(bf16)
    for k in range(1, NZ):
        z_copy(k).start()

    feature_ref[...] = nn(received(3), s.pack[0]).astype(bf16).T

    for k in range(1, NZ):
        z_copy(k).wait_recv()
    total = s.part[my_z].astype(f32)
    for k in range(1, NZ):
        total = total + s.grads_z[k].astype(f32)
    dqkv_ref[...] = total[:8, : 3 * D]
    dproj_ref[...] = total[:8, 3 * D : FF]
    dexpand_ref[...] = total[8:, :FF]
    dcontract_ref[:16, :] = total[:, FF : FF + D]
    dcontract_ref[16:, :] = total[:, FF + D : FF + 2 * D]
    gain_ref[...] = total[:8, FF + 2 * D :].T[:2, :]

    loop(lambda k: ask_copy(k, me).wait_send())
    for e in range(4):
        loop(lambda k: row_copy(e, k, me).wait_send())
    for k in range(1, NX):
        x_copy(k).wait_send()
    for k in range(1, NZ):
        z_copy(k).wait_send()


def per_device(features, morton_order, hilbert_order, cotangent, gains, qkv, proj, expand, contract):
    vmem = pl.BlockSpec(memory_space=pltpu.VMEM)
    shapes = [((N, D), bf16), ((N, D), bf16), ((2, 8), f32), ((8, 3 * D), f32), ((8, D), f32), ((8, FF), f32), ((32, D), f32)]
    return pl.pallas_call(
        kernel,
        out_shape=tuple(jax.ShapeDtypeStruct(*shape) for shape in shapes),
        in_specs=[vmem] * 9,
        out_specs=(vmem,) * 7,
        scratch_shapes=list(SCRATCH.values()),
        compiler_params=pltpu.CompilerParams(
            collective_id=0, has_side_effects=True, vmem_limit_bytes=60 << 20
        ),
    )(morton_order.reshape(1, N), hilbert_order.reshape(1, N), features, cotangent, gains, qkv, proj, expand, contract)


def solution(mesh):
    rows = P(("dp", "pts"), None)
    order = P(("dp", "pts"))
    return jax.shard_map(
        per_device,
        mesh=mesh,
        in_specs=(rows, order, order, rows, P(), P(), P(), P(), P()),
        out_specs=(rows, rows, P("dp", "pts"), rows, rows, rows, rows),
        check_vma=False,
    )
```

```python
import functools
import math

import jax
import jax.numpy as jnp
from jax import lax
from jax.experimental import pallas as pl
from jax.experimental.pallas import tpu as pltpu
from jax.sharding import PartitionSpec as P

f32, bf16 = jnp.float32, jnp.bfloat16
MESH = pl.DeviceIdType.MESH
D, HEADS, FF, HD = 256, 8, 1024, 32
N = 512
NX, NZ = 4, 8
PEERS = NX * NZ
SLOT = 32
SLOTS = PEERS * SLOT
WIDE = (1024, 640)
SCALE = HD**-0.5
LOG2E = math.log2(math.e)


def nn(a, b):
    return jnp.dot(a, b, preferred_element_type=f32)


def nt(a, b):
    return lax.dot_general(a, b, (((1,), (1,)), ((), ())), preferred_element_type=f32)


def iota(shape, axis):
    return lax.broadcasted_iota(jnp.int32, shape, axis)


def one_hot(condition):
    return jnp.where(condition, 1.0, 0.0).astype(bf16)


def norm_stats(x):
    center = x - jnp.mean(x, axis=0, keepdims=True)
    r = lax.rsqrt(jnp.mean(center * center, axis=0, keepdims=True) + 1e-5)
    return center * r, r


def norm_back(dn, xh, r, gain):
    dxh = dn * gain
    m1 = jnp.mean(dxh, axis=0, keepdims=True)
    m2 = jnp.mean(dxh * xh, axis=0, keepdims=True)
    return r * (dxh - m1 - xh * m2)


def heads_loop(head, per=4):
    def body(i, c):
        for k in range(per):
            head(i * per + k)
        return c

    lax.fori_loop(0, HEADS // per, body, 0)


def forward(x, s, b):
    xh, r = norm_stats(x)
    s.xh1[b] = xh
    s.r1[b] = r
    n1 = (xh * s.gain[2 * b][:, 0:1]).astype(bf16)
    s.n1[b] = n1
    s.qkv[b] = nn(s.qkv_t[b], n1).astype(bf16)
    s.kv[b] = nn(n1.T, s.qkv_w[b][:, D:]).astype(bf16)

    def head(h):
        rows = pl.multiple_of(h * HD, HD)
        keys = s.kv[b, :, :D] * s.mask[pl.ds(h, 1), :].astype(bf16)
        scores = nn(keys, s.qkv[b, :D, :])
        e = jnp.exp2(scores * (SCALE * LOG2E))
        p = (e * (1.0 / jnp.sum(e, axis=0, keepdims=True))).astype(bf16)
        s.attn[b, h] = p
        s.mix[b, pl.ds(rows, HD), :] = nn(s.qkv[b, pl.ds(rows + 2 * D, HD), :], p).astype(bf16)

    heads_loop(head)
    a = x + nn(s.proj_t[b], s.mix[b])
    xh2, r2 = norm_stats(a)
    s.xh2[b] = xh2
    s.r2[b] = r2
    n2 = (xh2 * s.gain[2 * b + 1][:, 0:1]).astype(bf16)
    s.n2[b] = n2
    u = nn(s.exp_t[b], n2)
    cdf = 0.5 + 0.5 * lax.erf(u * (0.5**0.5))
    hid = (u * cdf).astype(bf16)
    s.u[b] = u
    s.cdf[b] = cdf
    s.hid[b] = hid
    return (a + nn(s.con_t[b], hid)).astype(bf16)


def gelu_slope(s, b):
    u = s.u[b]
    s.u[b] = s.cdf[b] + u * (jnp.exp2(u * u * (-0.5 * LOG2E)) * (1 / math.sqrt(2 * math.pi)))


def fold(grad):
    half = grad.shape[1] // 2
    left, right = grad[:, :half].reshape(PEERS, 8, half), grad[:, half:].reshape(PEERS, 8, half)
    return jnp.concatenate([left, right], axis=1).astype(bf16)


def mlp_grads(dy, s):
    s.grads_a[:, :, :N] = fold(nt(s.n2[1], s.du[...]))
    contract = nt(s.hid[1], dy).astype(bf16).reshape(PEERS, 32, D)
    s.grads_a[:, :, N : N + D] = contract[:, :16]
    s.grads_a[:, :, N + D :] = contract[:, 16:]


def attention_grads(s):
    s.grads_b[:, :, :N] = fold(jnp.concatenate([nt(s.n1[1], s.dqkv[...]), nt(s.mix[1], s.dab[...])], axis=1))
    g1 = jnp.sum(s.dn1[...] * s.xh1[1], axis=1, keepdims=True)
    g2 = jnp.sum(s.dn2[...] * s.xh2[1], axis=1, keepdims=True)
    lane = iota((D, 256), 1)
    s.grads_b[:, :, N:] = fold(jnp.where(lane == 0, g1, jnp.where(lane == 1, g2, 0.0)))


def backward(dy, s, b, after_mlp=None):
    du = (nn(s.con_w[b], dy).astype(bf16).astype(f32) * s.u[b]).astype(bf16)
    s.du[...] = du
    if after_mlp is not None:
        after_mlp()
    dn2 = nn(s.exp_w[b], s.du[...]).astype(bf16).astype(f32)
    s.dn2[...] = dn2
    da = dy.astype(f32) + norm_back(dn2, s.xh2[b], s.r2[b], s.gain[2 * b + 1][:, 0:1])
    s.da[...] = da
    dab = da.astype(bf16)
    s.dab[...] = dab
    s.dmix[...] = nn(s.proj_w[b], dab).astype(bf16)

    def head(h):
        rows = pl.multiple_of(h * HD, HD)
        do = s.dmix[pl.ds(rows, HD), :]
        mixed = s.mix[b, pl.ds(rows, HD), :].astype(f32)
        delta = jnp.sum(do.astype(f32) * mixed, axis=0, keepdims=True)
        p = s.attn[b, h]
        values = s.kv[b, :, D:] * s.mask[pl.ds(h, 1), :].astype(bf16)
        ds = (p.astype(f32) * (nn(values, s.dmix[...]) - delta)).astype(bf16)
        query, key = s.qkv[b, pl.ds(rows, HD), :], s.qkv[b, pl.ds(rows + D, HD), :]
        s.dqkv[pl.ds(rows + 2 * D, HD), :] = nt(do, p).astype(bf16)
        s.dqkv[pl.ds(rows + D, HD), :] = (nt(query, ds) * SCALE).astype(bf16)
        s.dqkv[pl.ds(rows, HD), :] = (nn(key, ds) * SCALE).astype(bf16)

    heads_loop(head)
    dn1 = nn(s.qkv_w[b], s.dqkv[...]).astype(bf16).astype(f32)
    s.dn1[...] = dn1
    return (s.da[...] + norm_back(dn1, s.xh1[b], s.r1[b], s.gain[2 * b][:, 0:1])).astype(bf16)


def plan(order, shift):
    source, local = order >> 9, order & (N - 1)
    member = one_hot(source == iota((PEERS, N), 0))
    before = one_hot(iota((N, N), 0) < iota((N, N), 1))
    rank = jnp.sum(member.astype(f32) * nn(member, before), axis=0, keepdims=True).astype(jnp.int32)
    at_slot = one_hot(rank + shift == iota((128, N), 0))
    wanted = local + 1
    high, low = (wanted >> 8).astype(f32).astype(bf16), (wanted & 255).astype(f32).astype(bf16)
    asked = nt(member * high, at_slot) * 256.0 + nt(member * low, at_slot)
    return source * SLOT + rank, asked


def pack_matrix(asked, shift):
    at = iota((PEERS, SLOT, 128), 2) == iota((PEERS, SLOT, 128), 1) + shift
    column = jnp.sum(jnp.where(at, asked, 0.0), axis=2, keepdims=True).astype(jnp.int32)
    return one_hot(column == iota((PEERS, SLOT, N), 2) + 1).reshape(SLOTS, N)


class State:
    pass


SCRATCH = dict(
    mask=pltpu.VMEM((HEADS, D), f32),
    gain=pltpu.VMEM((4, D, 128), f32),
    xh1=pltpu.VMEM((2, D, N), f32),
    r1=pltpu.VMEM((2, 1, N), f32),
    xh2=pltpu.VMEM((2, D, N), f32),
    r2=pltpu.VMEM((2, 1, N), f32),
    n1=pltpu.VMEM((2, D, N), bf16),
    n2=pltpu.VMEM((2, D, N), bf16),
    qkv=pltpu.VMEM((2, 3 * D, N), bf16),
    kv=pltpu.VMEM((2, N, 2 * D), bf16),
    attn=pltpu.VMEM((2, HEADS, N, N), bf16),
    mix=pltpu.VMEM((2, D, N), bf16),
    u=pltpu.VMEM((2, FF, N), f32),
    cdf=pltpu.VMEM((2, FF, N), f32),
    hid=pltpu.VMEM((2, FF, N), bf16),
    du=pltpu.VMEM((FF, N), bf16),
    dab=pltpu.VMEM((D, N), bf16),
    dn1=pltpu.VMEM((D, N), f32),
    dn2=pltpu.VMEM((D, N), f32),
    dmix=pltpu.VMEM((D, N), bf16),
    dqkv=pltpu.VMEM((3 * D, N), bf16),
    qkv_t=pltpu.VMEM((2, 3 * D, D), bf16),
    proj_t=pltpu.VMEM((2, D, D), bf16),
    exp_t=pltpu.VMEM((2, FF, D), bf16),
    con_t=pltpu.VMEM((2, D, FF), bf16),
    cot_t=pltpu.VMEM((D, N), bf16),
    out_t=pltpu.VMEM((D, N), bf16),
    rows_t=pltpu.VMEM((D, N), bf16),
    grad_t=pltpu.VMEM((D, N), bf16),
    orders=pltpu.VMEM((2, 1, N), jnp.int32),
    gains=pltpu.VMEM((2, 2, D), bf16),
    pack=pltpu.VMEM((2, SLOTS, N), bf16),
    place=pltpu.VMEM((2, SLOTS, N), bf16),
    ask_out=pltpu.VMEM((PEERS, 1, 128), f32),
    ask_in=pltpu.VMEM((PEERS, 1, 128), f32),
    out=pltpu.VMEM((4, PEERS, SLOT, D), bf16),
    inc=pltpu.VMEM((4, PEERS, SLOT, D), bf16),
    da=pltpu.VMEM((D, N), f32),
    qkv_w=pltpu.VMEM((2, D, 3 * D), bf16),
    proj_w=pltpu.VMEM((2, D, D), bf16),
    exp_w=pltpu.VMEM((2, D, FF), bf16),
    con_w=pltpu.VMEM((2, FF, D), bf16),
    rows_in=pltpu.VMEM((N, D), bf16),
    cot=pltpu.VMEM((N, D), bf16),
    grads_a=pltpu.VMEM((PEERS, 16, WIDE[0]), bf16),
    grads_b=pltpu.VMEM((PEERS, 16, WIDE[1]), bf16),
    from_x_a=pltpu.VMEM((NX, NZ, 16, WIDE[0]), bf16),
    from_x_b=pltpu.VMEM((NX, NZ, 16, WIDE[1]), bf16),
    part_a=pltpu.VMEM((NZ, 16, WIDE[0]), bf16),
    part_b=pltpu.VMEM((NZ, 16, WIDE[1]), bf16),
    from_z_a=pltpu.VMEM((NZ, 16, WIDE[0]), bf16),
    from_z_b=pltpu.VMEM((NZ, 16, WIDE[1]), bf16),
    load=pltpu.SemaphoreType.DMA((9,)),
    ask_send=pltpu.SemaphoreType.DMA((PEERS,)),
    ask_recv=pltpu.SemaphoreType.DMA((PEERS,)),
    row_send=pltpu.SemaphoreType.DMA((4, PEERS)),
    row_recv=pltpu.SemaphoreType.DMA((4, PEERS)),
    x_send=pltpu.SemaphoreType.DMA((2, NX)),
    x_recv=pltpu.SemaphoreType.DMA((2, NX)),
    z_send=pltpu.SemaphoreType.DMA((2, NZ)),
    z_recv=pltpu.SemaphoreType.DMA((2, NZ)),
)


def kernel(
    morton_ref,
    hilbert_ref,
    features_ref,
    cotangent_ref,
    gains_ref,
    qkv_ref,
    proj_ref,
    expand_ref,
    contract_ref,
    block_ref,
    feature_ref,
    gain_ref,
    dqkv_ref,
    dproj_ref,
    dexpand_ref,
    dcontract_ref,
    *scratch,
):
    s = State()
    for name, ref in zip(SCRATCH, scratch):
        setattr(s, name, ref)
    me = lax.axis_index("pts")
    my_x, my_z = me // NZ, me % NZ

    def toward(k):
        return lax.rem(my_x + k // NZ, NX) * NZ + lax.rem(my_z + k % NZ, NZ)

    def origin(k):
        return toward((NX - k // NZ) % NX * NZ + (NZ - k % NZ) % NZ)

    def loop(body, order=range(1, PEERS)):
        for k in order:
            body(k)

    def copy(src, dst, send_sem, recv_sem, to):
        return pltpu.make_async_remote_copy(
            src_ref=src,
            dst_ref=dst,
            send_sem=send_sem,
            recv_sem=recv_sem,
            device_id={"pts": to},
            device_id_type=MESH,
        )

    def ask_copy(k, slot):
        to = toward(k)
        return copy(s.ask_out.at[to], s.ask_in.at[slot], s.ask_send.at[k], s.ask_recv.at[k], to)

    def row_copy(e, k, slot):
        to = toward(k)
        return copy(s.out.at[e, to], s.inc.at[e, slot], s.row_send.at[e, k], s.row_recv.at[e, k], to)

    def send_rows(e, matrix, pack):
        for dx in range(NX):
            first = pl.multiple_of(lax.rem(my_x + dx, NX) * NZ, NZ)
            rows = pack(matrix[pl.ds(pl.multiple_of(first * SLOT, SLOT), NZ * SLOT), :])
            s.out[e, pl.ds(first, NZ)] = rows.astype(bf16).reshape(NZ, SLOT, D)
            for k in range(max(dx * NZ, 1), (dx + 1) * NZ):
                row_copy(e, k, me).start()
        s.inc[e, me] = s.out[e, me]

    def received(e, matrix):
        total = None
        for dx in range(NX):
            for k in range(max(dx * NZ, 1), (dx + 1) * NZ):
                row_copy(e, k, origin(k)).wait_recv()
            first = pl.multiple_of(lax.rem(my_x + (NX - dx) % NX, NX) * NZ, NZ)
            rows = s.inc[e, pl.ds(first, NZ)].reshape(NZ * SLOT, D).T
            term = nn(rows, matrix[pl.ds(pl.multiple_of(first * SLOT, SLOT), NZ * SLOT), :])
            total = term if total is None else total + term
        return total

    barrier = pltpu.get_barrier_semaphore()
    loop(lambda k: pl.semaphore_signal(barrier, inc=1, device_id={"pts": toward(k)}, device_id_type=MESH))

    loads = (
        (morton_ref, s.orders.at[0]),
        (hilbert_ref, s.orders.at[1]),
        (features_ref, s.rows_in),
        (gains_ref, s.gains),
        (cotangent_ref, s.cot),
        (qkv_ref, s.qkv_w),
        (proj_ref, s.proj_w),
        (expand_ref, s.exp_w),
        (contract_ref, s.con_w),
    )
    loads = [pltpu.make_async_copy(src, dst, s.load.at[i]) for i, (src, dst) in enumerate(loads)]
    for one in loads:
        one.start()

    places = []
    asked = jnp.zeros((PEERS, 128), f32)
    for i in range(2):
        loads[i].wait()
        place, wanted = plan(s.orders[i], i * SLOT)
        places.append(place)
        asked = asked + wanted
    for p in range(PEERS):
        s.ask_out[p] = asked[p : p + 1, :]
    pl.semaphore_wait(barrier, PEERS - 1)
    loop(lambda k: ask_copy(k, me).start())
    s.ask_in[me] = s.ask_out[me]

    for i in range(2):
        s.place[i] = one_hot(places[i] == iota((SLOTS, N), 0))
    s.mask[...] = jnp.where(iota((HEADS, D), 1) // HD == iota((HEADS, D), 0), 1.0, 0.0)
    loads[3].wait()
    for i in range(4):
        row = s.gains[i // 2, i % 2 : i % 2 + 1, :].astype(f32)
        s.gain[i] = jnp.broadcast_to(row, (128, D)).T

    loop(lambda k: ask_copy(k, origin(k)).wait_recv())
    s.pack[0] = pack_matrix(s.ask_in[...], 0)
    loads[2].wait()
    send_rows(0, s.pack.at[0], lambda m: nn(m, s.rows_in[...]))
    for one in loads[4:]:
        one.wait()
    for b in range(2):
        s.qkv_t[b] = s.qkv_w[b].T
        s.proj_t[b] = s.proj_w[b].T
        s.exp_t[b] = s.exp_w[b].T
        s.con_t[b] = s.con_w[b].T
    s.pack[1] = pack_matrix(s.ask_in[...], SLOT)
    s.cot_t[...] = s.cot[...].T

    morton_rows = received(0, s.place.at[0])
    s.rows_t[...] = forward(morton_rows, s, 0)
    send_rows(1, s.pack.at[1], lambda m: nt(m, s.rows_t[...]))
    gelu_slope(s, 0)

    hilbert_rows = received(1, s.place.at[1])
    s.out_t[...] = forward(hilbert_rows, s, 1)
    gelu_slope(s, 1)

    grads, from_x = (s.grads_a, s.grads_b), (s.from_x_a, s.from_x_b)
    part, from_z = (s.part_a, s.part_b), (s.from_z_a, s.from_z_b)

    def x_copy(i, k):
        x = (my_x + k) % NX
        slab = grads[i].at[pl.ds(pl.multiple_of(x * NZ, NZ), NZ)]
        return copy(slab, from_x[i].at[k], s.x_send.at[i, k], s.x_recv.at[i, k], x * NZ + my_z)

    def z_copy(i, k):
        z = (my_z + k) % NZ
        return copy(part[i].at[z], from_z[i].at[k], s.z_send.at[i, k], s.z_recv.at[i, k], my_x * NZ + z)

    def along_x(i):
        for k in range(1, NX):
            x_copy(i, k).start()

    def along_z(i):
        for k in range(1, NX):
            x_copy(i, k).wait_recv()
        total = grads[i][pl.ds(pl.multiple_of(my_x * NZ, NZ), NZ)].astype(f32)
        for k in range(1, NX):
            total = total + from_x[i][k].astype(f32)
        part[i][...] = total.astype(bf16)
        for k in range(1, NZ):
            z_copy(i, k).start()

    def summed(i):
        for k in range(1, NZ):
            z_copy(i, k).wait_recv()
        total = part[i][my_z].astype(f32)
        for k in range(1, NZ):
            total = total + from_z[i][k].astype(f32)
        return total

    def send_mlp_grads():
        mlp_grads(s.cot_t[...], s)
        along_x(0)

    s.rows_t[...] = backward(s.cot_t[...], s, 1, send_mlp_grads)
    send_rows(2, s.place.at[1], lambda m: nt(m, s.rows_t[...]))
    block_ref[...] = s.out_t[...].T
    attention_grads(s)

    s.grad_t[...] = received(2, s.pack.at[1]).astype(bf16)
    along_x(1)
    along_z(0)
    s.rows_t[...] = backward(s.grad_t[...], s, 0)
    send_rows(3, s.place.at[0], lambda m: nt(m, s.rows_t[...]))
    along_z(1)

    feature_ref[...] = received(3, s.pack.at[0]).astype(bf16).T
    total = summed(0)
    dexpand_ref[:, :N] = total[:8, :N]
    dexpand_ref[:, N:] = total[8:, :N]
    dcontract_ref[:16, :] = total[:, N : N + D]
    dcontract_ref[16:, :] = total[:, N + D :]
    total = summed(1)
    dqkv_ref[:, :N] = total[:8, :N]
    dqkv_ref[:, N:] = total[8:, :D]
    dproj_ref[...] = total[8:, D:N]
    gain_ref[...] = total[:8, N:].T[:2, :]

    loop(lambda k: ask_copy(k, me).wait_send())
    for e in range(4):
        loop(lambda k: row_copy(e, k, me).wait_send())
    for i in range(2):
        for k in range(1, NX):
            x_copy(i, k).wait_send()
        for k in range(1, NZ):
            z_copy(i, k).wait_send()


def hand_on(*refs):
    for source, target in zip(refs[:7], refs[7:]):
        target[...] = source[...]


def per_device(features, morton_order, hilbert_order, cotangent, gains, qkv, proj, expand, contract):
    vmem, hbm = pl.BlockSpec(memory_space=pltpu.VMEM), pl.BlockSpec(memory_space=pl.ANY)
    shapes = [((N, D), bf16), ((N, D), bf16), ((2, 8), f32), ((8, 3 * D), f32), ((8, D), f32), ((8, FF), f32), ((32, D), f32)]
    shapes = tuple(jax.ShapeDtypeStruct(*shape) for shape in shapes)
    results = pl.pallas_call(
        kernel,
        out_shape=shapes,
        in_specs=[hbm] * 9,
        out_specs=(vmem,) * 7,
        scratch_shapes=list(SCRATCH.values()),
        compiler_params=pltpu.CompilerParams(
            collective_id=0, has_side_effects=True, vmem_limit_bytes=60 << 20
        ),
    )(morton_order.reshape(1, N), hilbert_order.reshape(1, N), features, cotangent, gains, qkv, proj, expand, contract)
    return pl.pallas_call(
        hand_on,
        out_shape=shapes,
        in_specs=[vmem] * 7,
        out_specs=(vmem,) * 7,
    )(*results)


def solution(mesh):
    rows = P(("dp", "pts"), None)
    order = P(("dp", "pts"))
    return jax.shard_map(
        per_device,
        mesh=mesh,
        in_specs=(rows, order, order, rows, P(), P(), P(), P(), P()),
        out_specs=(rows, rows, P("dp", "pts"), rows, rows, rows, rows),
        check_vma=False,
    )
```

```python
import functools
import math

import jax
import jax.numpy as jnp
from jax import lax
from jax.experimental import pallas as pl
from jax.experimental.pallas import tpu as pltpu
from jax.sharding import PartitionSpec as P

f32, bf16 = jnp.float32, jnp.bfloat16
MESH = pl.DeviceIdType.MESH
D, HEADS, FF, HD = 256, 8, 1024, 32
N = 512
NX, NZ = 4, 8
PEERS = NX * NZ
SLOT = 32
SLOTS = PEERS * SLOT
WIDE = (1024, 640)
X_ORDER, Z_ORDER = (2, 1, 3, 0), (4, 3, 5, 2, 6, 1, 7, 0)
GROUPS = [[dx * NZ + dz for dz in Z_ORDER if dx or dz] for dx in X_ORDER]
SCALE = HD**-0.5
LOG2E = math.log2(math.e)


def nn(a, b):
    return jnp.dot(a, b, preferred_element_type=f32)


def nt(a, b):
    return lax.dot_general(a, b, (((1,), (1,)), ((), ())), preferred_element_type=f32)


def iota(shape, axis):
    return lax.broadcasted_iota(jnp.int32, shape, axis)


def one_hot(condition):
    return jnp.where(condition, 1.0, 0.0).astype(bf16)


def norm_stats(x):
    center = x - jnp.mean(x, axis=0, keepdims=True)
    r = lax.rsqrt(jnp.mean(center * center, axis=0, keepdims=True) + 1e-5)
    return center * r, r


def norm_back(dn, xh, r, gain):
    dxh = dn * gain
    m1 = jnp.mean(dxh, axis=0, keepdims=True)
    m2 = jnp.mean(dxh * xh, axis=0, keepdims=True)
    return r * (dxh - m1 - xh * m2)


def heads_loop(head, per=4):
    def body(i, c):
        for k in range(per):
            head(i * per + k)
        return c

    lax.fori_loop(0, HEADS // per, body, 0)


def forward(x, s, b):
    xh, r = norm_stats(x)
    s.xh1[b] = xh
    s.r1[b] = r
    n1 = (xh * s.gain[2 * b][:, 0:1]).astype(bf16)
    s.n1[b] = n1
    s.qkv[b] = nn(s.qkv_t[b], n1).astype(bf16)
    s.kv[b] = nn(n1.T, s.qkv_w[b][:, D:]).astype(bf16)

    def head(h):
        rows = pl.multiple_of(h * HD, HD)
        keys = s.kv[b, :, :D] * s.mask[pl.ds(h, 1), :].astype(bf16)
        scores = nn(keys, s.qkv[b, :D, :])
        e = jnp.exp2(scores * (SCALE * LOG2E))
        p = (e * (1.0 / jnp.sum(e, axis=0, keepdims=True))).astype(bf16)
        s.attn[b, h] = p
        s.mix[b, pl.ds(rows, HD), :] = nn(s.qkv[b, pl.ds(rows + 2 * D, HD), :], p).astype(bf16)

    heads_loop(head)
    a = x + nn(s.proj_t[b], s.mix[b])
    xh2, r2 = norm_stats(a)
    s.xh2[b] = xh2
    s.r2[b] = r2
    n2 = (xh2 * s.gain[2 * b + 1][:, 0:1]).astype(bf16)
    s.n2[b] = n2
    u = nn(s.exp_t[b], n2)
    cdf = 0.5 + 0.5 * lax.erf(u * (0.5**0.5))
    hid = (u * cdf).astype(bf16)
    s.u[b] = u
    s.cdf[b] = cdf
    s.hid[b] = hid
    return (a + nn(s.con_t[b], hid)).astype(bf16)


def gelu_slope(s, b):
    u = s.u[b]
    s.u[b] = s.cdf[b] + u * (jnp.exp2(u * u * (-0.5 * LOG2E)) * (1 / math.sqrt(2 * math.pi)))


def fold(grad):
    half = grad.shape[1] // 2
    left, right = grad[:, :half].reshape(PEERS, 8, half), grad[:, half:].reshape(PEERS, 8, half)
    return jnp.concatenate([left, right], axis=1).astype(bf16)


def mlp_grads(dy, s):
    s.grads_a[:, :, :N] = fold(nt(s.n2[1], s.du[...]))
    contract = nt(s.hid[1], dy).astype(bf16).reshape(PEERS, 32, D)
    s.grads_a[:, :, N : N + D] = contract[:, :16]
    s.grads_a[:, :, N + D :] = contract[:, 16:]


def attention_grads(s):
    s.grads_b[:, :, :N] = fold(jnp.concatenate([nt(s.n1[1], s.dqkv[...]), nt(s.mix[1], s.dab[...])], axis=1))
    g1 = jnp.sum(s.dn1[...] * s.xh1[1], axis=1, keepdims=True)
    g2 = jnp.sum(s.dn2[...] * s.xh2[1], axis=1, keepdims=True)
    lane = iota((D, 256), 1)
    s.grads_b[:, :, N:] = fold(jnp.where(lane == 0, g1, jnp.where(lane == 1, g2, 0.0)))


def backward(dy, s, b, after_mlp=None):
    du = (nn(s.con_w[b], dy).astype(bf16).astype(f32) * s.u[b]).astype(bf16)
    s.du[...] = du
    if after_mlp is not None:
        after_mlp()
    dn2 = nn(s.exp_w[b], s.du[...]).astype(bf16).astype(f32)
    s.dn2[...] = dn2
    da = dy.astype(f32) + norm_back(dn2, s.xh2[b], s.r2[b], s.gain[2 * b + 1][:, 0:1])
    s.da[...] = da
    dab = da.astype(bf16)
    s.dab[...] = dab
    s.dmix[...] = nn(s.proj_w[b], dab).astype(bf16)

    def head(h):
        rows = pl.multiple_of(h * HD, HD)
        do = s.dmix[pl.ds(rows, HD), :]
        mixed = s.mix[b, pl.ds(rows, HD), :].astype(f32)
        delta = jnp.sum(do.astype(f32) * mixed, axis=0, keepdims=True)
        p = s.attn[b, h]
        values = s.kv[b, :, D:] * s.mask[pl.ds(h, 1), :].astype(bf16)
        ds = (p.astype(f32) * (nn(values, s.dmix[...]) - delta)).astype(bf16)
        query, key = s.qkv[b, pl.ds(rows, HD), :], s.qkv[b, pl.ds(rows + D, HD), :]
        s.dqkv[pl.ds(rows + 2 * D, HD), :] = nt(do, p).astype(bf16)
        s.dqkv[pl.ds(rows + D, HD), :] = (nt(query, ds) * SCALE).astype(bf16)
        s.dqkv[pl.ds(rows, HD), :] = (nn(key, ds) * SCALE).astype(bf16)

    heads_loop(head)
    dn1 = nn(s.qkv_w[b], s.dqkv[...]).astype(bf16).astype(f32)
    s.dn1[...] = dn1
    return (s.da[...] + norm_back(dn1, s.xh1[b], s.r1[b], s.gain[2 * b][:, 0:1])).astype(bf16)


def plan(order, shift):
    source, local = order >> 9, order & (N - 1)
    member = one_hot(source == iota((PEERS, N), 0))
    before = one_hot(iota((N, N), 0) < iota((N, N), 1))
    rank = jnp.sum(member.astype(f32) * nn(member, before), axis=0, keepdims=True).astype(jnp.int32)
    at_slot = one_hot(rank + shift == iota((128, N), 0))
    wanted = local + 1
    high, low = (wanted >> 8).astype(f32).astype(bf16), (wanted & 255).astype(f32).astype(bf16)
    asked = nt(member * high, at_slot) * 256.0 + nt(member * low, at_slot)
    return source * SLOT + rank, asked


def pack_matrix(asked, shift):
    at = iota((PEERS, SLOT, 128), 2) == iota((PEERS, SLOT, 128), 1) + shift
    column = jnp.sum(jnp.where(at, asked, 0.0), axis=2, keepdims=True).astype(jnp.int32)
    return one_hot(column == iota((PEERS, SLOT, N), 2) + 1).reshape(SLOTS, N)


class State:
    pass


SCRATCH = dict(
    mask=pltpu.VMEM((HEADS, D), f32),
    gain=pltpu.VMEM((4, D, 128), f32),
    xh1=pltpu.VMEM((2, D, N), f32),
    r1=pltpu.VMEM((2, 1, N), f32),
    xh2=pltpu.VMEM((2, D, N), f32),
    r2=pltpu.VMEM((2, 1, N), f32),
    n1=pltpu.VMEM((2, D, N), bf16),
    n2=pltpu.VMEM((2, D, N), bf16),
    qkv=pltpu.VMEM((2, 3 * D, N), bf16),
    kv=pltpu.VMEM((2, N, 2 * D), bf16),
    attn=pltpu.VMEM((2, HEADS, N, N), bf16),
    mix=pltpu.VMEM((2, D, N), bf16),
    u=pltpu.VMEM((2, FF, N), f32),
    cdf=pltpu.VMEM((2, FF, N), f32),
    hid=pltpu.VMEM((2, FF, N), bf16),
    du=pltpu.VMEM((FF, N), bf16),
    dab=pltpu.VMEM((D, N), bf16),
    dn1=pltpu.VMEM((D, N), f32),
    dn2=pltpu.VMEM((D, N), f32),
    dmix=pltpu.VMEM((D, N), bf16),
    dqkv=pltpu.VMEM((3 * D, N), bf16),
    qkv_t=pltpu.VMEM((2, 3 * D, D), bf16),
    proj_t=pltpu.VMEM((2, D, D), bf16),
    exp_t=pltpu.VMEM((2, FF, D), bf16),
    con_t=pltpu.VMEM((2, D, FF), bf16),
    cot_t=pltpu.VMEM((D, N), bf16),
    out_t=pltpu.VMEM((D, N), bf16),
    rows_t=pltpu.VMEM((D, N), bf16),
    grad_t=pltpu.VMEM((D, N), bf16),
    orders=pltpu.VMEM((2, 1, N), jnp.int32),
    gains=pltpu.VMEM((2, 2, D), bf16),
    pack=pltpu.VMEM((2, SLOTS, N), bf16),
    place=pltpu.VMEM((2, SLOTS, N), bf16),
    ask_out=pltpu.VMEM((PEERS, 1, 128), f32),
    ask_in=pltpu.VMEM((PEERS, 1, 128), f32),
    out=pltpu.VMEM((4, PEERS, SLOT, D), bf16),
    inc=pltpu.VMEM((4, PEERS, SLOT, D), bf16),
    da=pltpu.VMEM((D, N), f32),
    qkv_w=pltpu.VMEM((2, D, 3 * D), bf16),
    proj_w=pltpu.VMEM((2, D, D), bf16),
    exp_w=pltpu.VMEM((2, D, FF), bf16),
    con_w=pltpu.VMEM((2, FF, D), bf16),
    rows_in=pltpu.VMEM((N, D), bf16),
    cot=pltpu.VMEM((N, D), bf16),
    grads_a=pltpu.VMEM((PEERS, 16, WIDE[0]), bf16),
    grads_b=pltpu.VMEM((PEERS, 16, WIDE[1]), bf16),
    from_x_a=pltpu.VMEM((NX, NZ, 16, WIDE[0]), bf16),
    from_x_b=pltpu.VMEM((NX, NZ, 16, WIDE[1]), bf16),
    part_a=pltpu.VMEM((NZ, 16, WIDE[0]), bf16),
    part_b=pltpu.VMEM((NZ, 16, WIDE[1]), bf16),
    from_z_a=pltpu.VMEM((NZ, 16, WIDE[0]), bf16),
    from_z_b=pltpu.VMEM((NZ, 16, WIDE[1]), bf16),
    load=pltpu.SemaphoreType.DMA((9,)),
    ask_send=pltpu.SemaphoreType.DMA((PEERS,)),
    ask_recv=pltpu.SemaphoreType.DMA((PEERS,)),
    row_send=pltpu.SemaphoreType.DMA((4, PEERS)),
    row_recv=pltpu.SemaphoreType.DMA((4, PEERS)),
    x_send=pltpu.SemaphoreType.DMA((2, NX)),
    x_recv=pltpu.SemaphoreType.DMA((2, NX)),
    z_send=pltpu.SemaphoreType.DMA((2, NZ)),
    z_recv=pltpu.SemaphoreType.DMA((2, NZ)),
)


def kernel(
    morton_ref,
    hilbert_ref,
    features_ref,
    cotangent_ref,
    gains_ref,
    qkv_ref,
    proj_ref,
    expand_ref,
    contract_ref,
    block_ref,
    feature_ref,
    gain_ref,
    dqkv_ref,
    dproj_ref,
    dexpand_ref,
    dcontract_ref,
    *scratch,
):
    s = State()
    for name, ref in zip(SCRATCH, scratch):
        setattr(s, name, ref)
    me = lax.axis_index("pts")
    my_x, my_z = me // NZ, me % NZ

    def toward(k):
        return lax.rem(my_x + k // NZ, NX) * NZ + lax.rem(my_z + k % NZ, NZ)

    def origin(k):
        return toward((NX - k // NZ) % NX * NZ + (NZ - k % NZ) % NZ)

    def loop(body):
        for group in GROUPS:
            for k in group:
                body(k)

    def copy(src, dst, send_sem, recv_sem, to):
        return pltpu.make_async_remote_copy(
            src_ref=src,
            dst_ref=dst,
            send_sem=send_sem,
            recv_sem=recv_sem,
            device_id={"pts": to},
            device_id_type=MESH,
        )

    def ask_copy(k, slot):
        to = toward(k)
        return copy(s.ask_out.at[to], s.ask_in.at[slot], s.ask_send.at[k], s.ask_recv.at[k], to)

    def row_copy(e, k, slot):
        to = toward(k)
        return copy(s.out.at[e, to], s.inc.at[e, slot], s.row_send.at[e, k], s.row_recv.at[e, k], to)

    def send_rows(e, matrix, pack):
        for dx, group in zip(X_ORDER, GROUPS):
            first = pl.multiple_of(lax.rem(my_x + dx, NX) * NZ, NZ)
            rows = pack(matrix[pl.ds(pl.multiple_of(first * SLOT, SLOT), NZ * SLOT), :])
            s.out[e, pl.ds(first, NZ)] = rows.astype(bf16).reshape(NZ, SLOT, D)
            for k in group:
                row_copy(e, k, me).start()
        s.inc[e, me] = s.out[e, me]

    def sent(e):
        loop(lambda k: row_copy(e, k, me).wait_send())

    def received(e, matrix):
        total = None
        for dx, group in zip(X_ORDER, GROUPS):
            for k in group:
                row_copy(e, k, origin(k)).wait_recv()
            first = pl.multiple_of(lax.rem(my_x + (NX - dx) % NX, NX) * NZ, NZ)
            rows = s.inc[e, pl.ds(first, NZ)].reshape(NZ * SLOT, D).T
            term = nn(rows, matrix[pl.ds(pl.multiple_of(first * SLOT, SLOT), NZ * SLOT), :])
            total = term if total is None else total + term
        return total

    barrier = pltpu.get_barrier_semaphore()
    loop(lambda k: pl.semaphore_signal(barrier, inc=1, device_id={"pts": toward(k)}, device_id_type=MESH))

    loads = (
        (morton_ref, s.orders.at[0]),
        (hilbert_ref, s.orders.at[1]),
        (features_ref, s.rows_in),
        (gains_ref, s.gains),
        (cotangent_ref, s.cot),
        (qkv_ref, s.qkv_w),
        (proj_ref, s.proj_w),
        (expand_ref, s.exp_w),
        (contract_ref, s.con_w),
    )
    loads = [pltpu.make_async_copy(src, dst, s.load.at[i]) for i, (src, dst) in enumerate(loads)]
    for one in loads:
        one.start()

    places = []
    asked = jnp.zeros((PEERS, 128), f32)
    for i in range(2):
        loads[i].wait()
        place, wanted = plan(s.orders[i], i * SLOT)
        places.append(place)
        asked = asked + wanted
    for p in range(PEERS):
        s.ask_out[p] = asked[p : p + 1, :]
    pl.semaphore_wait(barrier, PEERS - 1)
    loop(lambda k: ask_copy(k, me).start())
    s.ask_in[me] = s.ask_out[me]

    for i in range(2):
        s.place[i] = one_hot(places[i] == iota((SLOTS, N), 0))
    s.mask[...] = jnp.where(iota((HEADS, D), 1) // HD == iota((HEADS, D), 0), 1.0, 0.0)
    loads[3].wait()
    for i in range(4):
        row = s.gains[i // 2, i % 2 : i % 2 + 1, :].astype(f32)
        s.gain[i] = jnp.broadcast_to(row, (128, D)).T

    loop(lambda k: ask_copy(k, origin(k)).wait_recv())
    s.pack[0] = pack_matrix(s.ask_in[...], 0)
    loads[2].wait()
    send_rows(0, s.pack.at[0], lambda m: nn(m, s.rows_in[...]))
    for one in loads[4:]:
        one.wait()
    for b in range(2):
        s.qkv_t[b] = s.qkv_w[b].T
        s.proj_t[b] = s.proj_w[b].T
        s.exp_t[b] = s.exp_w[b].T
        s.con_t[b] = s.con_w[b].T
    s.pack[1] = pack_matrix(s.ask_in[...], SLOT)
    s.cot_t[...] = s.cot[...].T
    loop(lambda k: ask_copy(k, me).wait_send())

    morton_rows = received(0, s.place.at[0])
    s.rows_t[...] = forward(morton_rows, s, 0)
    send_rows(1, s.pack.at[1], lambda m: nt(m, s.rows_t[...]))
    gelu_slope(s, 0)
    sent(0)

    hilbert_rows = received(1, s.place.at[1])
    s.out_t[...] = forward(hilbert_rows, s, 1)
    gelu_slope(s, 1)

    grads, from_x = (s.grads_a, s.grads_b), (s.from_x_a, s.from_x_b)
    part, from_z = (s.part_a, s.part_b), (s.from_z_a, s.from_z_b)

    def x_copy(i, k):
        x = (my_x + k) % NX
        slab = grads[i].at[pl.ds(pl.multiple_of(x * NZ, NZ), NZ)]
        return copy(slab, from_x[i].at[k], s.x_send.at[i, k], s.x_recv.at[i, k], x * NZ + my_z)

    def z_copy(i, k):
        z = (my_z + k) % NZ
        return copy(part[i].at[z], from_z[i].at[k], s.z_send.at[i, k], s.z_recv.at[i, k], my_x * NZ + z)

    def along_x(i):
        for k in range(1, NX):
            x_copy(i, k).start()

    def along_z(i):
        for k in range(1, NX):
            x_copy(i, k).wait_recv()
        total = grads[i][pl.ds(pl.multiple_of(my_x * NZ, NZ), NZ)].astype(f32)
        for k in range(1, NX):
            total = total + from_x[i][k].astype(f32)
        part[i][...] = total.astype(bf16)
        for k in range(1, NZ):
            z_copy(i, k).start()

    def summed(i):
        for k in range(1, NZ):
            z_copy(i, k).wait_recv()
        total = part[i][my_z].astype(f32)
        for k in range(1, NZ):
            total = total + from_z[i][k].astype(f32)
        return total

    def send_mlp_grads():
        mlp_grads(s.cot_t[...], s)
        along_x(0)

    s.rows_t[...] = backward(s.cot_t[...], s, 1, send_mlp_grads)
    send_rows(2, s.place.at[1], lambda m: nt(m, s.rows_t[...]))
    block_ref[...] = s.out_t[...].T
    attention_grads(s)
    sent(1)

    s.grad_t[...] = received(2, s.pack.at[1]).astype(bf16)
    along_x(1)
    along_z(0)
    s.rows_t[...] = backward(s.grad_t[...], s, 0)
    send_rows(3, s.place.at[0], lambda m: nt(m, s.rows_t[...]))
    along_z(1)
    sent(2)

    feature_ref[...] = received(3, s.pack.at[0]).astype(bf16).T
    total = summed(0)
    dexpand_ref[:, :N] = total[:8, :N]
    dexpand_ref[:, N:] = total[8:, :N]
    dcontract_ref[:16, :] = total[:, N : N + D]
    dcontract_ref[16:, :] = total[:, N + D :]
    total = summed(1)
    dqkv_ref[:, :N] = total[:8, :N]
    dqkv_ref[:, N:] = total[8:, :D]
    dproj_ref[...] = total[8:, D:N]
    gain_ref[...] = total[:8, N:].T[:2, :]

    sent(3)
    for i in range(2):
        for k in range(1, NX):
            x_copy(i, k).wait_send()
        for k in range(1, NZ):
            z_copy(i, k).wait_send()


def hand_on(*refs):
    for source, target in zip(refs[:7], refs[7:]):
        target[...] = source[...]


def per_device(features, morton_order, hilbert_order, cotangent, gains, qkv, proj, expand, contract):
    vmem, hbm = pl.BlockSpec(memory_space=pltpu.VMEM), pl.BlockSpec(memory_space=pl.ANY)
    shapes = [((N, D), bf16), ((N, D), bf16), ((2, 8), f32), ((8, 3 * D), f32), ((8, D), f32), ((8, FF), f32), ((32, D), f32)]
    shapes = tuple(jax.ShapeDtypeStruct(*shape) for shape in shapes)
    results = pl.pallas_call(
        kernel,
        out_shape=shapes,
        in_specs=[hbm] * 9,
        out_specs=(vmem,) * 7,
        scratch_shapes=list(SCRATCH.values()),
        compiler_params=pltpu.CompilerParams(
            collective_id=0, has_side_effects=True, vmem_limit_bytes=60 << 20
        ),
    )(morton_order.reshape(1, N), hilbert_order.reshape(1, N), features, cotangent, gains, qkv, proj, expand, contract)
    return pl.pallas_call(
        hand_on,
        out_shape=shapes,
        in_specs=[vmem] * 7,
        out_specs=(vmem,) * 7,
    )(*results)


def solution(mesh):
    rows = P(("dp", "pts"), None)
    order = P(("dp", "pts"))
    return jax.shard_map(
        per_device,
        mesh=mesh,
        in_specs=(rows, order, order, rows, P(), P(), P(), P(), P()),
        out_specs=(rows, rows, P("dp", "pts"), rows, rows, rows, rows),
        check_vma=False,
    )
```

```python
import functools
import math

import jax
import jax.numpy as jnp
from jax import lax
from jax.experimental import pallas as pl
from jax.experimental.pallas import tpu as pltpu
from jax.sharding import PartitionSpec as P

f32, bf16 = jnp.float32, jnp.bfloat16
MESH = pl.DeviceIdType.MESH
D, HEADS, FF, HD = 256, 8, 1024, 32
N = 512
NX, NZ = 4, 8
PEERS = NX * NZ
SLOT = 32
SLOTS = PEERS * SLOT
WIDE = (1024, 640)
X_ORDER, Z_ORDER = (2, 1, 3, 0), (4, 3, 5, 2, 6, 1, 7, 0)
GROUPS = [[dx * NZ + dz for dz in Z_ORDER if dx or dz] for dx in X_ORDER]
SCALE = HD**-0.5
LOG2E = math.log2(math.e)


def nn(a, b):
    return jnp.dot(a, b, preferred_element_type=f32)


def nt(a, b):
    return lax.dot_general(a, b, (((1,), (1,)), ((), ())), preferred_element_type=f32)


def iota(shape, axis):
    return lax.broadcasted_iota(jnp.int32, shape, axis)


def one_hot(condition):
    return jnp.where(condition, 1.0, 0.0).astype(bf16)


def norm_stats(x):
    center = x - jnp.mean(x, axis=0, keepdims=True)
    r = lax.rsqrt(jnp.mean(center * center, axis=0, keepdims=True) + 1e-5)
    return center * r, r


def norm_back(dn, xh, r, gain):
    dxh = dn * gain
    m1 = jnp.mean(dxh, axis=0, keepdims=True)
    m2 = jnp.mean(dxh * xh, axis=0, keepdims=True)
    return r * (dxh - m1 - xh * m2)


def heads_loop(head, per=4):
    def body(i, c):
        for k in range(per):
            head(i * per + k)
        return c

    lax.fori_loop(0, HEADS // per, body, 0)


def forward(x, s, b):
    xh, r = norm_stats(x)
    s.xh1[b] = xh
    s.r1[b] = r
    n1 = (xh * s.gain[2 * b][:, 0:1]).astype(bf16)
    s.n1[b] = n1
    s.qkv[b] = nn(s.qkv_t[b], n1).astype(bf16)
    s.kv[b] = nn(n1.T, s.qkv_w[b][:, D:]).astype(bf16)

    def head(h):
        rows = pl.multiple_of(h * HD, HD)
        keys = s.kv[b, :, :D] * s.mask[pl.ds(h, 1), :].astype(bf16)
        scores = nn(keys, s.qkv[b, :D, :])
        e = jnp.exp2(scores * (SCALE * LOG2E))
        p = (e * (1.0 / jnp.sum(e, axis=0, keepdims=True))).astype(bf16)
        s.attn[b, h] = p
        s.mix[b, pl.ds(rows, HD), :] = nn(s.qkv[b, pl.ds(rows + 2 * D, HD), :], p).astype(bf16)

    heads_loop(head)
    a = x + nn(s.proj_t[b], s.mix[b])
    xh2, r2 = norm_stats(a)
    s.xh2[b] = xh2
    s.r2[b] = r2
    n2 = (xh2 * s.gain[2 * b + 1][:, 0:1]).astype(bf16)
    s.n2[b] = n2
    u = nn(s.exp_t[b], n2)
    cdf = 0.5 + 0.5 * lax.erf(u * (0.5**0.5))
    hid = (u * cdf).astype(bf16)
    s.hid[b] = hid
    if b == 0:
        s.u[...] = u
        s.cdf[...] = cdf
        return (a + nn(s.con_t[b], hid)).astype(bf16)
    s.du[...] = (s.dhid[...].astype(f32) * gelu_slope(u, cdf)).astype(bf16)
    s.after[...] = a


def gelu_slope(u, cdf):
    return cdf + u * (jnp.exp2(u * u * (-0.5 * LOG2E)) * (1 / math.sqrt(2 * math.pi)))


def fold(grad):
    half = grad.shape[1] // 2
    left, right = grad[:, :half].reshape(PEERS, 8, half), grad[:, half:].reshape(PEERS, 8, half)
    return jnp.concatenate([left, right], axis=1).astype(bf16)


def mlp_grads(dy, s):
    s.grads_a[:, :, :N] = fold(nt(s.n2[1], s.du[...]))
    contract = nt(s.hid[1], dy).astype(bf16).reshape(PEERS, 32, D)
    s.grads_a[:, :, N : N + D] = contract[:, :16]
    s.grads_a[:, :, N + D :] = contract[:, 16:]


def attention_grads(s):
    s.grads_b[:, :, :N] = fold(jnp.concatenate([nt(s.n1[1], s.dqkv[...]), nt(s.mix[1], s.dab[...])], axis=1))
    g1 = jnp.sum(s.dn1[...] * s.xh1[1], axis=1, keepdims=True)
    g2 = jnp.sum(s.dn2[...] * s.xh2[1], axis=1, keepdims=True)
    lane = iota((D, 256), 1)
    s.grads_b[:, :, N:] = fold(jnp.where(lane == 0, g1, jnp.where(lane == 1, g2, 0.0)))


def backward(dy, s, b, after_mlp=None):
    if b == 0:
        s.du[...] = (nn(s.con_w[b], dy).astype(bf16).astype(f32) * s.u[...]).astype(bf16)
    if after_mlp is not None:
        after_mlp()
    dn2 = nn(s.exp_w[b], s.du[...]).astype(bf16).astype(f32)
    s.dn2[...] = dn2
    da = dy.astype(f32) + norm_back(dn2, s.xh2[b], s.r2[b], s.gain[2 * b + 1][:, 0:1])
    s.da[...] = da
    dab = da.astype(bf16)
    s.dab[...] = dab
    s.dmix[...] = nn(s.proj_w[b], dab).astype(bf16)

    def head(h):
        rows = pl.multiple_of(h * HD, HD)
        do = s.dmix[pl.ds(rows, HD), :]
        mixed = s.mix[b, pl.ds(rows, HD), :].astype(f32)
        delta = jnp.sum(do.astype(f32) * mixed, axis=0, keepdims=True)
        p = s.attn[b, h]
        values = s.kv[b, :, D:] * s.mask[pl.ds(h, 1), :].astype(bf16)
        ds = (p.astype(f32) * (nn(values, s.dmix[...]) - delta)).astype(bf16)
        query, key = s.qkv[b, pl.ds(rows, HD), :], s.qkv[b, pl.ds(rows + D, HD), :]
        s.dqkv[pl.ds(rows + 2 * D, HD), :] = nt(do, p).astype(bf16)
        s.dqkv[pl.ds(rows + D, HD), :] = (nt(query, ds) * SCALE).astype(bf16)
        s.dqkv[pl.ds(rows, HD), :] = (nn(key, ds) * SCALE).astype(bf16)

    heads_loop(head)
    dn1 = nn(s.qkv_w[b], s.dqkv[...]).astype(bf16).astype(f32)
    s.dn1[...] = dn1
    return (s.da[...] + norm_back(dn1, s.xh1[b], s.r1[b], s.gain[2 * b][:, 0:1])).astype(bf16)


def plan(order, shift):
    source, local = order >> 9, order & (N - 1)
    member = one_hot(source == iota((PEERS, N), 0))
    before = one_hot(iota((N, N), 0) < iota((N, N), 1))
    rank = jnp.sum(member.astype(f32) * nn(member, before), axis=0, keepdims=True).astype(jnp.int32)
    at_slot = one_hot(rank + shift == iota((128, N), 0))
    wanted = local + 1
    high, low = (wanted >> 8).astype(f32).astype(bf16), (wanted & 255).astype(f32).astype(bf16)
    asked = nt(member * high, at_slot) * 256.0 + nt(member * low, at_slot)
    return source * SLOT + rank, asked


def pack_matrix(asked, shift):
    at = iota((PEERS, SLOT, 128), 2) == iota((PEERS, SLOT, 128), 1) + shift
    column = jnp.sum(jnp.where(at, asked, 0.0), axis=2, keepdims=True).astype(jnp.int32)
    return one_hot(column == iota((PEERS, SLOT, N), 2) + 1).reshape(SLOTS, N)


class State:
    pass


SCRATCH = dict(
    mask=pltpu.VMEM((HEADS, D), f32),
    gain=pltpu.VMEM((4, D, 128), f32),
    xh1=pltpu.VMEM((2, D, N), f32),
    r1=pltpu.VMEM((2, 1, N), f32),
    xh2=pltpu.VMEM((2, D, N), f32),
    r2=pltpu.VMEM((2, 1, N), f32),
    n1=pltpu.VMEM((2, D, N), bf16),
    n2=pltpu.VMEM((2, D, N), bf16),
    qkv=pltpu.VMEM((2, 3 * D, N), bf16),
    kv=pltpu.VMEM((2, N, 2 * D), bf16),
    attn=pltpu.VMEM((2, HEADS, N, N), bf16),
    mix=pltpu.VMEM((2, D, N), bf16),
    u=pltpu.VMEM((FF, N), f32),
    cdf=pltpu.VMEM((FF, N), f32),
    after=pltpu.VMEM((D, N), f32),
    dhid=pltpu.VMEM((FF, N), bf16),
    hid=pltpu.VMEM((2, FF, N), bf16),
    du=pltpu.VMEM((FF, N), bf16),
    dab=pltpu.VMEM((D, N), bf16),
    dn1=pltpu.VMEM((D, N), f32),
    dn2=pltpu.VMEM((D, N), f32),
    dmix=pltpu.VMEM((D, N), bf16),
    dqkv=pltpu.VMEM((3 * D, N), bf16),
    qkv_t=pltpu.VMEM((2, 3 * D, D), bf16),
    proj_t=pltpu.VMEM((2, D, D), bf16),
    exp_t=pltpu.VMEM((2, FF, D), bf16),
    con_t=pltpu.VMEM((2, D, FF), bf16),
    cot_t=pltpu.VMEM((D, N), bf16),
    rows_t=pltpu.VMEM((D, N), bf16),
    grad_t=pltpu.VMEM((D, N), bf16),
    orders=pltpu.VMEM((2, 1, N), jnp.int32),
    gains=pltpu.VMEM((2, 2, D), bf16),
    pack=pltpu.VMEM((2, SLOTS, N), bf16),
    place=pltpu.VMEM((2, SLOTS, N), bf16),
    ask_out=pltpu.VMEM((PEERS, 1, 128), f32),
    ask_in=pltpu.VMEM((PEERS, 1, 128), f32),
    out=pltpu.VMEM((4, PEERS, SLOT, D), bf16),
    inc=pltpu.VMEM((4, PEERS, SLOT, D), bf16),
    da=pltpu.VMEM((D, N), f32),
    qkv_w=pltpu.VMEM((2, D, 3 * D), bf16),
    proj_w=pltpu.VMEM((2, D, D), bf16),
    exp_w=pltpu.VMEM((2, D, FF), bf16),
    con_w=pltpu.VMEM((2, FF, D), bf16),
    rows_in=pltpu.VMEM((N, D), bf16),
    cot=pltpu.VMEM((N, D), bf16),
    grads_a=pltpu.VMEM((PEERS, 16, WIDE[0]), bf16),
    grads_b=pltpu.VMEM((PEERS, 16, WIDE[1]), bf16),
    from_x_a=pltpu.VMEM((NX, NZ, 16, WIDE[0]), bf16),
    from_x_b=pltpu.VMEM((NX, NZ, 16, WIDE[1]), bf16),
    part_a=pltpu.VMEM((NZ, 16, WIDE[0]), bf16),
    part_b=pltpu.VMEM((NZ, 16, WIDE[1]), bf16),
    from_z_a=pltpu.VMEM((NZ, 16, WIDE[0]), bf16),
    from_z_b=pltpu.VMEM((NZ, 16, WIDE[1]), bf16),
    load=pltpu.SemaphoreType.DMA((9,)),
    ask_send=pltpu.SemaphoreType.DMA((PEERS,)),
    ask_recv=pltpu.SemaphoreType.DMA((PEERS,)),
    row_send=pltpu.SemaphoreType.DMA((4, PEERS)),
    row_recv=pltpu.SemaphoreType.DMA((4, PEERS)),
    x_send=pltpu.SemaphoreType.DMA((2, NX)),
    x_recv=pltpu.SemaphoreType.DMA((2, NX)),
    z_send=pltpu.SemaphoreType.DMA((2, NZ)),
    z_recv=pltpu.SemaphoreType.DMA((2, NZ)),
)


def kernel(
    morton_ref,
    hilbert_ref,
    features_ref,
    cotangent_ref,
    gains_ref,
    qkv_ref,
    proj_ref,
    expand_ref,
    contract_ref,
    block_ref,
    feature_ref,
    gain_ref,
    dqkv_ref,
    dproj_ref,
    dexpand_ref,
    dcontract_ref,
    *scratch,
):
    s = State()
    for name, ref in zip(SCRATCH, scratch):
        setattr(s, name, ref)
    me = lax.axis_index("pts")
    my_x, my_z = me // NZ, me % NZ

    def toward(k):
        return lax.rem(my_x + k // NZ, NX) * NZ + lax.rem(my_z + k % NZ, NZ)

    def origin(k):
        return toward((NX - k // NZ) % NX * NZ + (NZ - k % NZ) % NZ)

    def loop(body):
        for group in GROUPS:
            for k in group:
                body(k)

    def copy(src, dst, send_sem, recv_sem, to):
        return pltpu.make_async_remote_copy(
            src_ref=src,
            dst_ref=dst,
            send_sem=send_sem,
            recv_sem=recv_sem,
            device_id={"pts": to},
            device_id_type=MESH,
        )

    def ask_copy(k, slot):
        to = toward(k)
        return copy(s.ask_out.at[to], s.ask_in.at[slot], s.ask_send.at[k], s.ask_recv.at[k], to)

    def row_copy(e, k, slot):
        to = toward(k)
        return copy(s.out.at[e, to], s.inc.at[e, slot], s.row_send.at[e, k], s.row_recv.at[e, k], to)

    def send_rows(e, matrix, pack):
        for dx, group in zip(X_ORDER, GROUPS):
            first = pl.multiple_of(lax.rem(my_x + dx, NX) * NZ, NZ)
            rows = pack(matrix[pl.ds(pl.multiple_of(first * SLOT, SLOT), NZ * SLOT), :])
            s.out[e, pl.ds(first, NZ)] = rows.astype(bf16).reshape(NZ, SLOT, D)
            for k in group:
                row_copy(e, k, me).start()
        s.inc[e, me] = s.out[e, me]

    def sent(e):
        loop(lambda k: row_copy(e, k, me).wait_send())

    def received(e, matrix):
        total = None
        for dx, group in zip(X_ORDER, GROUPS):
            for k in group:
                row_copy(e, k, origin(k)).wait_recv()
            first = pl.multiple_of(lax.rem(my_x + (NX - dx) % NX, NX) * NZ, NZ)
            rows = s.inc[e, pl.ds(first, NZ)].reshape(NZ * SLOT, D).T
            term = nn(rows, matrix[pl.ds(pl.multiple_of(first * SLOT, SLOT), NZ * SLOT), :])
            total = term if total is None else total + term
        return total

    barrier = pltpu.get_barrier_semaphore()
    loop(lambda k: pl.semaphore_signal(barrier, inc=1, device_id={"pts": toward(k)}, device_id_type=MESH))

    loads = (
        (morton_ref, s.orders.at[0]),
        (hilbert_ref, s.orders.at[1]),
        (features_ref, s.rows_in),
        (gains_ref, s.gains),
        (cotangent_ref, s.cot),
        (qkv_ref, s.qkv_w),
        (proj_ref, s.proj_w),
        (expand_ref, s.exp_w),
        (contract_ref, s.con_w),
    )
    loads = [pltpu.make_async_copy(src, dst, s.load.at[i]) for i, (src, dst) in enumerate(loads)]
    for one in loads:
        one.start()

    places = []
    asked = jnp.zeros((PEERS, 128), f32)
    for i in range(2):
        loads[i].wait()
        place, wanted = plan(s.orders[i], i * SLOT)
        places.append(place)
        asked = asked + wanted
    for p in range(PEERS):
        s.ask_out[p] = asked[p : p + 1, :]
    pl.semaphore_wait(barrier, PEERS - 1)
    loop(lambda k: ask_copy(k, me).start())
    s.ask_in[me] = s.ask_out[me]

    for i in range(2):
        s.place[i] = one_hot(places[i] == iota((SLOTS, N), 0))
    s.mask[...] = jnp.where(iota((HEADS, D), 1) // HD == iota((HEADS, D), 0), 1.0, 0.0)
    loads[3].wait()
    for i in range(4):
        row = s.gains[i // 2, i % 2 : i % 2 + 1, :].astype(f32)
        s.gain[i] = jnp.broadcast_to(row, (128, D)).T

    loop(lambda k: ask_copy(k, origin(k)).wait_recv())
    s.pack[0] = pack_matrix(s.ask_in[...], 0)
    loads[2].wait()
    send_rows(0, s.pack.at[0], lambda m: nn(m, s.rows_in[...]))
    for one in loads[4:]:
        one.wait()
    for b in range(2):
        s.qkv_t[b] = s.qkv_w[b].T
        s.proj_t[b] = s.proj_w[b].T
        s.exp_t[b] = s.exp_w[b].T
        s.con_t[b] = s.con_w[b].T
    s.pack[1] = pack_matrix(s.ask_in[...], SLOT)
    s.cot_t[...] = s.cot[...].T
    loop(lambda k: ask_copy(k, me).wait_send())

    morton_rows = received(0, s.place.at[0])
    s.rows_t[...] = forward(morton_rows, s, 0)
    send_rows(1, s.pack.at[1], lambda m: nt(m, s.rows_t[...]))
    s.u[...] = gelu_slope(s.u[...], s.cdf[...])
    s.dhid[...] = nn(s.con_w[1], s.cot_t[...]).astype(bf16)
    sent(0)

    hilbert_rows = received(1, s.place.at[1])
    forward(hilbert_rows, s, 1)

    grads, from_x = (s.grads_a, s.grads_b), (s.from_x_a, s.from_x_b)
    part, from_z = (s.part_a, s.part_b), (s.from_z_a, s.from_z_b)

    def x_copy(i, k):
        x = (my_x + k) % NX
        slab = grads[i].at[pl.ds(pl.multiple_of(x * NZ, NZ), NZ)]
        return copy(slab, from_x[i].at[k], s.x_send.at[i, k], s.x_recv.at[i, k], x * NZ + my_z)

    def z_copy(i, k):
        z = (my_z + k) % NZ
        return copy(part[i].at[z], from_z[i].at[k], s.z_send.at[i, k], s.z_recv.at[i, k], my_x * NZ + z)

    def along_x(i):
        for k in range(1, NX):
            x_copy(i, k).start()

    def along_z(i):
        for k in range(1, NX):
            x_copy(i, k).wait_recv()
        total = grads[i][pl.ds(pl.multiple_of(my_x * NZ, NZ), NZ)].astype(f32)
        for k in range(1, NX):
            total = total + from_x[i][k].astype(f32)
        part[i][...] = total.astype(bf16)
        for k in range(1, NZ):
            z_copy(i, k).start()

    def summed(i):
        for k in range(1, NZ):
            z_copy(i, k).wait_recv()
        total = part[i][my_z].astype(f32)
        for k in range(1, NZ):
            total = total + from_z[i][k].astype(f32)
        return total

    def send_mlp_grads():
        mlp_grads(s.cot_t[...], s)
        along_x(0)

    s.rows_t[...] = backward(s.cot_t[...], s, 1, send_mlp_grads)
    send_rows(2, s.place.at[1], lambda m: nt(m, s.rows_t[...]))
    block_ref[...] = (s.after[...] + nn(s.con_t[1], s.hid[1])).astype(bf16).T
    attention_grads(s)
    sent(1)

    s.grad_t[...] = received(2, s.pack.at[1]).astype(bf16)
    along_x(1)
    along_z(0)
    s.rows_t[...] = backward(s.grad_t[...], s, 0)
    send_rows(3, s.place.at[0], lambda m: nt(m, s.rows_t[...]))
    along_z(1)
    sent(2)

    feature_ref[...] = received(3, s.pack.at[0]).astype(bf16).T
    total = summed(0)
    dexpand_ref[:, :N] = total[:8, :N]
    dexpand_ref[:, N:] = total[8:, :N]
    dcontract_ref[:16, :] = total[:, N : N + D]
    dcontract_ref[16:, :] = total[:, N + D :]
    total = summed(1)
    dqkv_ref[:, :N] = total[:8, :N]
    dqkv_ref[:, N:] = total[8:, :D]
    dproj_ref[...] = total[8:, D:N]
    gain_ref[...] = total[:8, N:].T[:2, :]

    sent(3)
    for i in range(2):
        for k in range(1, NX):
            x_copy(i, k).wait_send()
        for k in range(1, NZ):
            z_copy(i, k).wait_send()


def hand_on(*refs):
    for source, target in zip(refs[:7], refs[7:]):
        target[...] = source[...]


def per_device(features, morton_order, hilbert_order, cotangent, gains, qkv, proj, expand, contract):
    vmem, hbm = pl.BlockSpec(memory_space=pltpu.VMEM), pl.BlockSpec(memory_space=pl.ANY)
    shapes = [((N, D), bf16), ((N, D), bf16), ((2, 8), f32), ((8, 3 * D), f32), ((8, D), f32), ((8, FF), f32), ((32, D), f32)]
    shapes = tuple(jax.ShapeDtypeStruct(*shape) for shape in shapes)
    results = pl.pallas_call(
        kernel,
        out_shape=shapes,
        in_specs=[hbm] * 9,
        out_specs=(vmem,) * 7,
        scratch_shapes=list(SCRATCH.values()),
        compiler_params=pltpu.CompilerParams(
            collective_id=0, has_side_effects=True, vmem_limit_bytes=60 << 20
        ),
    )(morton_order.reshape(1, N), hilbert_order.reshape(1, N), features, cotangent, gains, qkv, proj, expand, contract)
    return pl.pallas_call(
        hand_on,
        out_shape=shapes,
        in_specs=[vmem] * 7,
        out_specs=(vmem,) * 7,
    )(*results)


def solution(mesh):
    rows = P(("dp", "pts"), None)
    order = P(("dp", "pts"))
    return jax.shard_map(
        per_device,
        mesh=mesh,
        in_specs=(rows, order, order, rows, P(), P(), P(), P(), P()),
        out_specs=(rows, rows, P("dp", "pts"), rows, rows, rows, rows),
        check_vma=False,
    )
```

```python
import functools
import math

import jax
import jax.numpy as jnp
from jax import lax
from jax.experimental import pallas as pl
from jax.experimental.pallas import tpu as pltpu
from jax.sharding import PartitionSpec as P

f32, bf16 = jnp.float32, jnp.bfloat16
MESH = pl.DeviceIdType.MESH
D, HEADS, FF, HD = 256, 8, 1024, 32
N = 512
NX, NZ = 4, 8
PEERS = NX * NZ
SLOT = 32
SLOTS = PEERS * SLOT
WIDE = (1024, 640)
X_ORDER, Z_ORDER = (2, 1, 3, 0), (4, 3, 5, 2, 6, 1, 7, 0)
GROUPS = [[dx * NZ + dz for dz in Z_ORDER if dx or dz] for dx in X_ORDER]
SCALE = HD**-0.5
LOG2E = math.log2(math.e)


def nn(a, b):
    return jnp.dot(a, b, preferred_element_type=f32)


def nt(a, b):
    return lax.dot_general(a, b, (((1,), (1,)), ((), ())), preferred_element_type=f32)


def iota(shape, axis):
    return lax.broadcasted_iota(jnp.int32, shape, axis)


def one_hot(condition):
    return jnp.where(condition, 1.0, 0.0).astype(bf16)


def norm_stats(x):
    center = x - jnp.mean(x, axis=0, keepdims=True)
    r = lax.rsqrt(jnp.mean(center * center, axis=0, keepdims=True) + 1e-5)
    return center * r, r


def norm_back(dn, xh, r, gain):
    dxh = dn * gain
    m1 = jnp.mean(dxh, axis=0, keepdims=True)
    m2 = jnp.mean(dxh * xh, axis=0, keepdims=True)
    return r * (dxh - m1 - xh * m2)


def heads_loop(head, per=4):
    def body(i, c):
        for k in range(per):
            head(i * per + k)
        return c

    lax.fori_loop(0, HEADS // per, body, 0)


def forward(x, s, b):
    xh, r = norm_stats(x)
    s.xh1[b] = xh
    s.r1[b] = r
    n1 = (xh * s.gain[2 * b][:, 0:1]).astype(bf16)
    s.n1[b] = n1
    s.qkv[b] = nn(s.qkv_t[b], n1).astype(bf16)
    s.kv[b] = nn(n1.T, s.qkv_w[b][:, D:]).astype(bf16)

    def head(h):
        rows = pl.multiple_of(h * HD, HD)
        keys = s.kv[b, :, :D] * s.mask[pl.ds(h, 1), :].astype(bf16)
        scores = nn(keys, s.qkv[b, :D, :])
        e = jnp.exp2(scores * (SCALE * LOG2E))
        p = (e * (1.0 / jnp.sum(e, axis=0, keepdims=True))).astype(bf16)
        s.attn[b, h] = p
        s.mix[b, pl.ds(rows, HD), :] = nn(s.qkv[b, pl.ds(rows + 2 * D, HD), :], p).astype(bf16)

    heads_loop(head)
    a = x + nn(s.proj_t[b], s.mix[b])
    xh2, r2 = norm_stats(a)
    s.xh2[b] = xh2
    s.r2[b] = r2
    n2 = (xh2 * s.gain[2 * b + 1][:, 0:1]).astype(bf16)
    s.n2[b] = n2
    u = nn(s.exp_t[b], n2)
    cdf = 0.5 + 0.5 * lax.erf(u * (0.5**0.5))
    hid = (u * cdf).astype(bf16)
    s.hid[b] = hid
    if b == 0:
        s.u[...] = u
        s.cdf[...] = cdf
        return (a + nn(s.con_t[b], hid)).astype(bf16)
    s.du[...] = (s.dhid[...].astype(f32) * gelu_slope(u, cdf)).astype(bf16)
    s.after[...] = a


def gelu_slope(u, cdf):
    return cdf + u * (jnp.exp2(u * u * (-0.5 * LOG2E)) * (1 / math.sqrt(2 * math.pi)))


def fold(grad):
    half = grad.shape[1] // 2
    left, right = grad[:, :half].reshape(PEERS, 8, half), grad[:, half:].reshape(PEERS, 8, half)
    return jnp.concatenate([left, right], axis=1).astype(bf16)


def mlp_grads(dy, s):
    s.grads_a[:, :, :N] = fold(nt(s.n2[1], s.du[...]))
    contract = nt(s.hid[1], dy).astype(bf16).reshape(PEERS, 32, D)
    s.grads_a[:, :, N : N + D] = contract[:, :16]
    s.grads_a[:, :, N + D :] = contract[:, 16:]


def attention_grads(s):
    s.grads_b[:, :, :N] = fold(jnp.concatenate([nt(s.n1[1], s.dqkv[...]), nt(s.mix[1], s.dab[...])], axis=1))
    g1 = jnp.sum(s.dn1[...] * s.xh1[1], axis=1, keepdims=True)
    g2 = jnp.sum(s.dn2[...] * s.xh2[1], axis=1, keepdims=True)
    lane = iota((D, 256), 1)
    s.grads_b[:, :, N:] = fold(jnp.where(lane == 0, g1, jnp.where(lane == 1, g2, 0.0)))


def backward(dy, s, b, after_mlp=None):
    if b == 0:
        s.du[...] = (nn(s.con_w[b], dy).astype(bf16).astype(f32) * s.u[...]).astype(bf16)
    if after_mlp is not None:
        after_mlp()
    dn2 = nn(s.exp_w[b], s.du[...]).astype(bf16).astype(f32)
    s.dn2[...] = dn2
    da = dy.astype(f32) + norm_back(dn2, s.xh2[b], s.r2[b], s.gain[2 * b + 1][:, 0:1])
    s.da[...] = da
    dab = da.astype(bf16)
    s.dab[...] = dab
    s.dmix[...] = nn(s.proj_w[b], dab).astype(bf16)

    def head(h):
        rows = pl.multiple_of(h * HD, HD)
        do = s.dmix[pl.ds(rows, HD), :]
        mixed = s.mix[b, pl.ds(rows, HD), :].astype(f32)
        delta = jnp.sum(do.astype(f32) * mixed, axis=0, keepdims=True)
        p = s.attn[b, h]
        values = s.kv[b, :, D:] * s.mask[pl.ds(h, 1), :].astype(bf16)
        ds = (p.astype(f32) * (nn(values, s.dmix[...]) - delta)).astype(bf16)
        query, key = s.qkv[b, pl.ds(rows, HD), :], s.qkv[b, pl.ds(rows + D, HD), :]
        s.dqkv[pl.ds(rows + 2 * D, HD), :] = nt(do, p).astype(bf16)
        s.dqkv[pl.ds(rows + D, HD), :] = (nt(query, ds) * SCALE).astype(bf16)
        s.dqkv[pl.ds(rows, HD), :] = (nn(key, ds) * SCALE).astype(bf16)

    heads_loop(head, HEADS)
    dn1 = nn(s.qkv_w[b], s.dqkv[...]).astype(bf16).astype(f32)
    s.dn1[...] = dn1
    return (s.da[...] + norm_back(dn1, s.xh1[b], s.r1[b], s.gain[2 * b][:, 0:1])).astype(bf16)


def plan(order, shift):
    source, local = order >> 9, order & (N - 1)
    member = one_hot(source == iota((PEERS, N), 0))
    before = one_hot(iota((N, N), 0) < iota((N, N), 1))
    rank = jnp.sum(member.astype(f32) * nn(member, before), axis=0, keepdims=True).astype(jnp.int32)
    at_slot = one_hot(rank + shift == iota((128, N), 0))
    wanted = local + 1
    high, low = (wanted >> 8).astype(f32).astype(bf16), (wanted & 255).astype(f32).astype(bf16)
    asked = nt(member * high, at_slot) * 256.0 + nt(member * low, at_slot)
    return source * SLOT + rank, asked


def pack_matrix(asked, shift):
    at = iota((PEERS, SLOT, 128), 2) == iota((PEERS, SLOT, 128), 1) + shift
    column = jnp.sum(jnp.where(at, asked, 0.0), axis=2, keepdims=True).astype(jnp.int32)
    return one_hot(column == iota((PEERS, SLOT, N), 2) + 1).reshape(SLOTS, N)


class State:
    pass


SCRATCH = dict(
    mask=pltpu.VMEM((HEADS, D), f32),
    gain=pltpu.VMEM((4, D, 128), f32),
    xh1=pltpu.VMEM((2, D, N), f32),
    r1=pltpu.VMEM((2, 1, N), f32),
    xh2=pltpu.VMEM((2, D, N), f32),
    r2=pltpu.VMEM((2, 1, N), f32),
    n1=pltpu.VMEM((2, D, N), bf16),
    n2=pltpu.VMEM((2, D, N), bf16),
    qkv=pltpu.VMEM((2, 3 * D, N), bf16),
    kv=pltpu.VMEM((2, N, 2 * D), bf16),
    attn=pltpu.VMEM((2, HEADS, N, N), bf16),
    mix=pltpu.VMEM((2, D, N), bf16),
    u=pltpu.VMEM((FF, N), f32),
    cdf=pltpu.VMEM((FF, N), f32),
    after=pltpu.VMEM((D, N), f32),
    dhid=pltpu.VMEM((FF, N), bf16),
    hid=pltpu.VMEM((2, FF, N), bf16),
    du=pltpu.VMEM((FF, N), bf16),
    dab=pltpu.VMEM((D, N), bf16),
    dn1=pltpu.VMEM((D, N), f32),
    dn2=pltpu.VMEM((D, N), f32),
    dmix=pltpu.VMEM((D, N), bf16),
    dqkv=pltpu.VMEM((3 * D, N), bf16),
    qkv_t=pltpu.VMEM((2, 3 * D, D), bf16),
    proj_t=pltpu.VMEM((2, D, D), bf16),
    exp_t=pltpu.VMEM((2, FF, D), bf16),
    con_t=pltpu.VMEM((2, D, FF), bf16),
    cot_t=pltpu.VMEM((D, N), bf16),
    rows_t=pltpu.VMEM((D, N), bf16),
    grad_t=pltpu.VMEM((D, N), bf16),
    orders=pltpu.VMEM((2, 1, N), jnp.int32),
    gains=pltpu.VMEM((2, 2, D), bf16),
    pack=pltpu.VMEM((2, SLOTS, N), bf16),
    place=pltpu.VMEM((2, SLOTS, N), bf16),
    ask_out=pltpu.VMEM((PEERS, 1, 128), f32),
    ask_in=pltpu.VMEM((PEERS, 1, 128), f32),
    out=pltpu.VMEM((4, PEERS, SLOT, D), bf16),
    inc=pltpu.VMEM((4, PEERS, SLOT, D), bf16),
    da=pltpu.VMEM((D, N), f32),
    qkv_w=pltpu.VMEM((2, D, 3 * D), bf16),
    proj_w=pltpu.VMEM((2, D, D), bf16),
    exp_w=pltpu.VMEM((2, D, FF), bf16),
    con_w=pltpu.VMEM((2, FF, D), bf16),
    rows_in=pltpu.VMEM((N, D), bf16),
    cot=pltpu.VMEM((N, D), bf16),
    grads_a=pltpu.VMEM((PEERS, 16, WIDE[0]), bf16),
    grads_b=pltpu.VMEM((PEERS, 16, WIDE[1]), bf16),
    from_x_a=pltpu.VMEM((NX, NZ, 16, WIDE[0]), bf16),
    from_x_b=pltpu.VMEM((NX, NZ, 16, WIDE[1]), bf16),
    part_a=pltpu.VMEM((NZ, 16, WIDE[0]), bf16),
    part_b=pltpu.VMEM((NZ, 16, WIDE[1]), bf16),
    from_z_a=pltpu.VMEM((NZ, 16, WIDE[0]), bf16),
    from_z_b=pltpu.VMEM((NZ, 16, WIDE[1]), bf16),
    load=pltpu.SemaphoreType.DMA((9,)),
    ask_send=pltpu.SemaphoreType.DMA((PEERS,)),
    ask_recv=pltpu.SemaphoreType.DMA((PEERS,)),
    row_send=pltpu.SemaphoreType.DMA((4, PEERS)),
    row_recv=pltpu.SemaphoreType.DMA((4, PEERS)),
    x_send=pltpu.SemaphoreType.DMA((2, NX)),
    x_recv=pltpu.SemaphoreType.DMA((2, NX)),
    z_send=pltpu.SemaphoreType.DMA((2, NZ)),
    z_recv=pltpu.SemaphoreType.DMA((2, NZ)),
)


def kernel(
    morton_ref,
    hilbert_ref,
    features_ref,
    cotangent_ref,
    gains_ref,
    qkv_ref,
    proj_ref,
    expand_ref,
    contract_ref,
    block_ref,
    feature_ref,
    gain_ref,
    dqkv_ref,
    dproj_ref,
    dexpand_ref,
    dcontract_ref,
    *scratch,
):
    s = State()
    for name, ref in zip(SCRATCH, scratch):
        setattr(s, name, ref)
    me = lax.axis_index("pts")
    my_x, my_z = me // NZ, me % NZ

    def toward(k):
        return lax.rem(my_x + k // NZ, NX) * NZ + lax.rem(my_z + k % NZ, NZ)

    def origin(k):
        return toward((NX - k // NZ) % NX * NZ + (NZ - k % NZ) % NZ)

    def loop(body):
        for group in GROUPS:
            for k in group:
                body(k)

    def copy(src, dst, send_sem, recv_sem, to):
        return pltpu.make_async_remote_copy(
            src_ref=src,
            dst_ref=dst,
            send_sem=send_sem,
            recv_sem=recv_sem,
            device_id={"pts": to},
            device_id_type=MESH,
        )

    def ask_copy(k, slot):
        to = toward(k)
        return copy(s.ask_out.at[to], s.ask_in.at[slot], s.ask_send.at[k], s.ask_recv.at[k], to)

    def row_copy(e, k, slot):
        to = toward(k)
        return copy(s.out.at[e, to], s.inc.at[e, slot], s.row_send.at[e, k], s.row_recv.at[e, k], to)

    def send_rows(e, matrix, pack):
        for dx, group in zip(X_ORDER, GROUPS):
            first = pl.multiple_of(lax.rem(my_x + dx, NX) * NZ, NZ)
            rows = pack(matrix[pl.ds(pl.multiple_of(first * SLOT, SLOT), NZ * SLOT), :])
            s.out[e, pl.ds(first, NZ)] = rows.astype(bf16).reshape(NZ, SLOT, D)
            for k in group:
                row_copy(e, k, me).start()
        s.inc[e, me] = s.out[e, me]

    def sent(e):
        loop(lambda k: row_copy(e, k, me).wait_send())

    def received(e, matrix):
        total = None
        for dx, group in zip(X_ORDER, GROUPS):
            for k in group:
                row_copy(e, k, origin(k)).wait_recv()
            first = pl.multiple_of(lax.rem(my_x + (NX - dx) % NX, NX) * NZ, NZ)
            rows = s.inc[e, pl.ds(first, NZ)].reshape(NZ * SLOT, D).T
            term = nn(rows, matrix[pl.ds(pl.multiple_of(first * SLOT, SLOT), NZ * SLOT), :])
            total = term if total is None else total + term
        return total

    barrier = pltpu.get_barrier_semaphore()
    loop(lambda k: pl.semaphore_signal(barrier, inc=1, device_id={"pts": toward(k)}, device_id_type=MESH))

    loads = (
        (morton_ref, s.orders.at[0]),
        (hilbert_ref, s.orders.at[1]),
        (features_ref, s.rows_in),
        (gains_ref, s.gains),
        (cotangent_ref, s.cot),
        (qkv_ref, s.qkv_w),
        (proj_ref, s.proj_w),
        (expand_ref, s.exp_w),
        (contract_ref, s.con_w),
    )
    loads = [pltpu.make_async_copy(src, dst, s.load.at[i]) for i, (src, dst) in enumerate(loads)]
    for one in loads:
        one.start()

    places = []
    asked = jnp.zeros((PEERS, 128), f32)
    for i in range(2):
        loads[i].wait()
        place, wanted = plan(s.orders[i], i * SLOT)
        places.append(place)
        asked = asked + wanted
    for p in range(PEERS):
        s.ask_out[p] = asked[p : p + 1, :]
    pl.semaphore_wait(barrier, PEERS - 1)
    loop(lambda k: ask_copy(k, me).start())
    s.ask_in[me] = s.ask_out[me]

    for i in range(2):
        s.place[i] = one_hot(places[i] == iota((SLOTS, N), 0))
    s.mask[...] = jnp.where(iota((HEADS, D), 1) // HD == iota((HEADS, D), 0), 1.0, 0.0)
    loads[3].wait()
    for i in range(4):
        row = s.gains[i // 2, i % 2 : i % 2 + 1, :].astype(f32)
        s.gain[i] = jnp.broadcast_to(row, (128, D)).T

    loop(lambda k: ask_copy(k, origin(k)).wait_recv())
    s.pack[0] = pack_matrix(s.ask_in[...], 0)
    loads[2].wait()
    send_rows(0, s.pack.at[0], lambda m: nn(m, s.rows_in[...]))
    for one in loads[4:]:
        one.wait()
    for b in range(2):
        s.qkv_t[b] = s.qkv_w[b].T
        s.proj_t[b] = s.proj_w[b].T
        s.exp_t[b] = s.exp_w[b].T
        s.con_t[b] = s.con_w[b].T
    s.pack[1] = pack_matrix(s.ask_in[...], SLOT)
    s.cot_t[...] = s.cot[...].T
    loop(lambda k: ask_copy(k, me).wait_send())

    morton_rows = received(0, s.place.at[0])
    s.rows_t[...] = forward(morton_rows, s, 0)
    send_rows(1, s.pack.at[1], lambda m: nt(m, s.rows_t[...]))
    s.u[...] = gelu_slope(s.u[...], s.cdf[...])
    s.dhid[...] = nn(s.con_w[1], s.cot_t[...]).astype(bf16)
    sent(0)

    hilbert_rows = received(1, s.place.at[1])
    forward(hilbert_rows, s, 1)

    grads, from_x = (s.grads_a, s.grads_b), (s.from_x_a, s.from_x_b)
    part, from_z = (s.part_a, s.part_b), (s.from_z_a, s.from_z_b)

    def x_copy(i, k):
        x = (my_x + k) % NX
        slab = grads[i].at[pl.ds(pl.multiple_of(x * NZ, NZ), NZ)]
        return copy(slab, from_x[i].at[k], s.x_send.at[i, k], s.x_recv.at[i, k], x * NZ + my_z)

    def z_copy(i, k):
        z = (my_z + k) % NZ
        return copy(part[i].at[z], from_z[i].at[k], s.z_send.at[i, k], s.z_recv.at[i, k], my_x * NZ + z)

    def along_x(i):
        for k in range(1, NX):
            x_copy(i, k).start()

    def along_z(i):
        for k in range(1, NX):
            x_copy(i, k).wait_recv()
        total = grads[i][pl.ds(pl.multiple_of(my_x * NZ, NZ), NZ)].astype(f32)
        for k in range(1, NX):
            total = total + from_x[i][k].astype(f32)
        part[i][...] = total.astype(bf16)
        for k in range(1, NZ):
            z_copy(i, k).start()

    def summed(i):
        for k in range(1, NZ):
            z_copy(i, k).wait_recv()
        total = part[i][my_z].astype(f32)
        for k in range(1, NZ):
            total = total + from_z[i][k].astype(f32)
        return total

    def send_mlp_grads():
        mlp_grads(s.cot_t[...], s)
        along_x(0)

    s.rows_t[...] = backward(s.cot_t[...], s, 1, send_mlp_grads)
    send_rows(2, s.place.at[1], lambda m: nt(m, s.rows_t[...]))
    block_ref[...] = (s.after[...] + nn(s.con_t[1], s.hid[1])).astype(bf16).T
    attention_grads(s)
    sent(1)

    s.grad_t[...] = received(2, s.pack.at[1]).astype(bf16)
    along_x(1)
    along_z(0)
    s.rows_t[...] = backward(s.grad_t[...], s, 0)
    send_rows(3, s.place.at[0], lambda m: nt(m, s.rows_t[...]))
    along_z(1)
    sent(2)

    feature_ref[...] = received(3, s.pack.at[0]).astype(bf16).T
    total = summed(0)
    dexpand_ref[:, :N] = total[:8, :N]
    dexpand_ref[:, N:] = total[8:, :N]
    dcontract_ref[:16, :] = total[:, N : N + D]
    dcontract_ref[16:, :] = total[:, N + D :]
    total = summed(1)
    dqkv_ref[:, :N] = total[:8, :N]
    dqkv_ref[:, N:] = total[8:, :D]
    dproj_ref[...] = total[8:, D:N]
    gain_ref[...] = total[:8, N:].T[:2, :]

    sent(3)
    for i in range(2):
        for k in range(1, NX):
            x_copy(i, k).wait_send()
        for k in range(1, NZ):
            z_copy(i, k).wait_send()


def hand_on(*refs):
    for source, target in zip(refs[:7], refs[7:]):
        target[...] = source[...]


def per_device(features, morton_order, hilbert_order, cotangent, gains, qkv, proj, expand, contract):
    vmem, hbm = pl.BlockSpec(memory_space=pltpu.VMEM), pl.BlockSpec(memory_space=pl.ANY)
    shapes = [((N, D), bf16), ((N, D), bf16), ((2, 8), f32), ((8, 3 * D), f32), ((8, D), f32), ((8, FF), f32), ((32, D), f32)]
    shapes = tuple(jax.ShapeDtypeStruct(*shape) for shape in shapes)
    results = pl.pallas_call(
        kernel,
        out_shape=shapes,
        in_specs=[hbm] * 9,
        out_specs=(vmem,) * 7,
        scratch_shapes=list(SCRATCH.values()),
        compiler_params=pltpu.CompilerParams(
            collective_id=0, has_side_effects=True, vmem_limit_bytes=60 << 20
        ),
    )(morton_order.reshape(1, N), hilbert_order.reshape(1, N), features, cotangent, gains, qkv, proj, expand, contract)
    return pl.pallas_call(
        hand_on,
        out_shape=shapes,
        in_specs=[vmem] * 7,
        out_specs=(vmem,) * 7,
    )(*results)


def solution(mesh):
    rows = P(("dp", "pts"), None)
    order = P(("dp", "pts"))
    return jax.shard_map(
        per_device,
        mesh=mesh,
        in_specs=(rows, order, order, rows, P(), P(), P(), P(), P()),
        out_specs=(rows, rows, P("dp", "pts"), rows, rows, rows, rows),
        check_vma=False,
    )
```
